32 devices in a mesh: ctx: 4 (over y, x), head: 8 (over z, core).
Axes of the slice: x: 2, y: 2, z: 4, core: 2. Of those that a mesh axis runs over, the one named last changes fastest.
Arguments:
- queries: bfloat16 [2, 2048, 2048], P(None, 'ctx', 'head'), may hold values from -6 to 6
- keys: bfloat16 [2, 2048, 2048], P(None, 'ctx', 'head'), may hold values from -6 to 6
- values: bfloat16 [2, 2048, 2048], P(None, 'ctx', 'head'), may hold values from -6 to 6
- rates: float32 [8, 2, 2048], P('head', None, 'ctx'), may hold values from 0.05 to 1
- w_gate: float32 [8, 256, 512], P('head'), may hold values from -0.375 to 0.375
- w_up: float32 [8, 256, 512], P('head'), may hold values from -0.375 to 0.375
- w_down: float32 [8, 512, 256], P('head'), may hold values from -0.25 to 0.25
- gains: float32 [8, 256], P('head'), may hold values from 0.25 to 0.6
- out_proj: bfloat16 [2048, 2048], P('head'), may hold values from -0.1875 to 0.1875
Outputs:
- output: bfloat16 [2, 2048, 2048], P(None, 'ctx', 'head')
The draws below stay inside these ranges and needn't reach their ends.
All inputs are finite; a program needn't handle non-finite values.
Results may differ from the reference program's by a relative error of at most 0.0051.
Values may be sent and summed in bfloat16 or wider, within the bound.
No kernel may reach another device: no remote copies, remote signals or barrier semaphores. Data moves between devices by JAX's collectives and lax.ppermute only.
A program may use at most 128 MiB of HBM per device.

```python
import math
import jax
import jax.numpy as jnp
from jax import lax

HD = 256
FH = 512
WINDOW = 256
NS_ITERS = 5
GROUPS = 2
HEADS = 8
D = 2048
GROUP_TOK = 2048


def raised(entries, stream_key, source, target, parts, factor):
    def block_of(position):
        return (jnp.arange(entries.shape[position]) // (entries.shape[position] // parts)).reshape((-1,) + (1,) * (entries.ndim - 1 - position))

    near = jax.random.permutation(stream_key, parts)[block_of(target)]
    second = (block_of(target) + parts // 2) % parts
    return jnp.where((block_of(source) == near) | (block_of(source) == second), factor * entries, entries)


def level_of(key, shape, cuts, low, high):
    def one(position, blocks):
        steps = jax.random.uniform(jax.random.fold_in(jax.random.fold_in(key, 6), position), (blocks,), jnp.float32, low / len(cuts), high / len(cuts))
        return jnp.repeat(jnp.exp(steps), shape[position] // blocks).reshape((-1,) + (1,) * (len(shape) - position - 1))

    level = one(*cuts[0])
    for cut in cuts[1:]:
        level = level * one(*cut)
    return level


def normal_values(rng, extent, spread, bound, cuts=(), kind=jnp.bfloat16):
    values = spread * jax.random.normal(rng, extent, jnp.float32)
    if cuts:
        values = values * level_of(rng, extent, cuts, -0.22, 0.18)
    return jnp.clip(values, -bound, bound).astype(kind)


def bell_draw_with(own_key, dims, scale, limit, cuts, heavy, kind=jnp.bfloat16):
    drawn = scale * jax.random.normal(own_key, dims, jnp.float32)
    if cuts:
        drawn = drawn * level_of(own_key, dims, cuts, -0.22, 0.18)
    return jnp.clip(raised(drawn, jax.random.fold_in(own_key, 3), *heavy), -limit, limit).astype(kind)


def setup_inputs(seed: int = 0) -> dict:
    key_of = jax.random.split(jax.random.key(seed), 10)
    return {
        "queries": normal_values(key_of[0], (GROUPS, GROUP_TOK, D), 1.0, 6.0, ((1, 4), (2, 8))),
        "keys": normal_values(key_of[1], (GROUPS, GROUP_TOK, D), 1.0, 6.0, ((1, 4), (2, 8))),
        "values": normal_values(key_of[2], (GROUPS, GROUP_TOK, D), 1.0, 6.0, ((1, 4), (2, 8))),
        "rates": jnp.clip(jnp.exp(math.log(1.0) - 2.9957323 * jax.random.uniform(key_of[3], (HEADS, GROUPS, GROUP_TOK), jnp.float32) ** level_of(key_of[3], (HEADS, GROUPS, GROUP_TOK), ((0, 8), (2, 4)), -0.2, 0.2)), 0.05, 1.0),
        "w_gate": normal_values(key_of[4], (HEADS, HD, FH), HD ** -0.5, 0.375, ((0, 8),), jnp.float32),
        "w_up": normal_values(key_of[5], (HEADS, HD, FH), HD ** -0.5, 0.375, ((0, 8),), jnp.float32),
        "w_down": normal_values(key_of[6], (HEADS, FH, HD), FH ** -0.5, 0.25, ((0, 8),), jnp.float32),
        "gains": jnp.clip(0.25 + 0.35000002 * jax.random.uniform(key_of[7], (HEADS, HD), jnp.float32) ** level_of(key_of[7], (HEADS, HD), ((0, 8),), -0.2, 0.2), 0.25, 0.6),
        "out_proj": bell_draw_with(key_of[8], (D, D), D ** -0.5, 0.1875, ((0, 8),), (0, 1, 8, 2.0)),
    }


highest = lax.Precision.HIGHEST
attn_temp = 5.0
step_size = 0.5
quintic_one = 3.4445
quintic_two = -4.775
quintic_three = 2.0315

def unit_rows(matrix):
    return matrix / jnp.sqrt(lax.optimization_barrier(jnp.sum(matrix * matrix, axis=-1, keepdims=True)) + 1e-06)

def exact_dot(left, right):
    return jnp.dot(left, right, precision=highest, preferred_element_type=jnp.float32)

def fast_grads(key_unit, value_rows, rate_rows, w_gate, w_up, w_down):
    gate_pre = exact_dot(key_unit, w_gate)
    up_pre = exact_dot(key_unit, w_up)
    sigma = jax.nn.sigmoid(gate_pre)
    gate_act = gate_pre * sigma
    hidden = gate_act * up_pre
    target = rate_rows[:, None] * value_rows
    grad_down = exact_dot(hidden.T, target)
    back_hidden = exact_dot(target, w_down.T)
    slope = sigma * (1.0 + gate_pre * (1.0 - sigma))
    grad_gate = exact_dot(key_unit.T, back_hidden * up_pre * slope)
    grad_up = exact_dot(key_unit.T, back_hidden * gate_act)
    return jnp.stack([grad_gate, grad_up, grad_down.T])

def orthogonal(grads):
    norms = jnp.sqrt(lax.optimization_barrier(jnp.sum(grads * grads, axis=(1, 2), keepdims=True))) + 1e-06
    iterate = grads / norms
    for sweep_at in range(NS_ITERS):
        gram = jnp.einsum('mik,mjk->mij', iterate, iterate, precision=highest)
        poly = quintic_two * gram + quintic_three * jnp.einsum('mij,mjk->mik', gram, gram, precision=highest)
        iterate = quintic_one * iterate + jnp.einsum('mij,mjk->mik', poly, iterate, precision=highest)
    return iterate

def apply_fast(query_unit, w_gate, w_up, w_down):
    gate_pre = exact_dot(query_unit, w_gate)
    gate_act = gate_pre * jax.nn.sigmoid(gate_pre)
    return exact_dot(gate_act * exact_dot(query_unit, w_up), w_down)

def window_attention(query_half, key_half, value_rows):
    total_rows = query_half.shape[0]
    key_pad = jnp.concatenate([jnp.zeros((WINDOW, HD), key_half.dtype), key_half], axis=0)
    value_pad = jnp.concatenate([jnp.zeros((WINDOW, HD), value_rows.dtype), value_rows], axis=0)

    def one_block(start):
        query_block = lax.dynamic_slice_in_dim(query_half, start, WINDOW, 0)
        key_block = lax.dynamic_slice_in_dim(key_pad, start, 2 * WINDOW, 0)
        value_block = lax.dynamic_slice_in_dim(value_pad, start, 2 * WINDOW, 0)
        scores = lax.dot_general(query_block, key_block, (((1,), (1,)), ((), ())), preferred_element_type=jnp.float32)
        query_pos = jnp.arange(WINDOW, dtype=jnp.int32)[:, None]
        key_pos = jnp.arange(2 * WINDOW, dtype=jnp.int32)[None, :]
        distance = query_pos + WINDOW - key_pos
        valid = (distance >= 0) & (distance < WINDOW) & (key_pos + start >= WINDOW)
        weights = jnp.where(valid, jnp.exp(attn_temp * (scores - 1.0)), 0.0)
        probs = (weights / lax.optimization_barrier(jnp.sum(weights, axis=-1, keepdims=True))).astype(jnp.bfloat16)
        return jnp.dot(probs, value_block, preferred_element_type=jnp.float32)
    starts = (jnp.arange(total_rows // WINDOW) * WINDOW).astype(jnp.int32)
    return lax.map(one_block, starts).reshape(total_rows, HD)

def head_path(operands):
    query_rows, key_rows, value_rows, rate_rows, gate_now, up_now, down_now, gain_row = operands
    query_unit = unit_rows(query_rows.astype(jnp.float32))
    key_unit = unit_rows(key_rows.astype(jnp.float32))
    attended = window_attention(query_unit.astype(jnp.bfloat16), key_unit.astype(jnp.bfloat16), value_rows)
    pieces = []
    for group_at in range(GROUPS):
        lower = group_at * GROUP_TOK
        upper = lower + GROUP_TOK
        grads = fast_grads(key_unit[lower:upper], value_rows[lower:upper].astype(jnp.float32), rate_rows[group_at], gate_now, up_now, down_now)
        ortho = orthogonal(grads)
        gate_now = gate_now + step_size * ortho[0]
        up_now = up_now + step_size * ortho[1]
        down_now = down_now + step_size * ortho[2].T
        pieces.append(apply_fast(query_unit[lower:upper], gate_now, up_now, down_now))
    fast_out = jnp.concatenate(pieces, axis=0)
    normed = fast_out * lax.rsqrt(lax.optimization_barrier(jnp.mean(fast_out * fast_out, axis=-1, keepdims=True)) + 1e-05) * gain_row
    return (attended + normed).astype(jnp.bfloat16)

def reference(queries, keys, values, rates, w_gate, w_up, w_down, gains, out_proj):
    total_rows = GROUPS * GROUP_TOK

    def to_heads(array):
        return array.reshape(total_rows, HEADS, HD).transpose(1, 0, 2)
    combined = lax.map(head_path, (to_heads(queries), to_heads(keys), to_heads(values), rates, w_gate, w_up, w_down, gains))
    flat = combined.transpose(1, 0, 2).reshape(total_rows, HEADS * HD)
    result = jnp.dot(flat, out_proj, preferred_element_type=jnp.float32).astype(jnp.bfloat16)
    return result.reshape(GROUPS, GROUP_TOK, D)
```

```python
import functools

import jax
import jax.numpy as jnp
from jax import lax
from jax.experimental import pallas as pl
from jax.experimental.pallas import tpu as pltpu
from jax.sharding import PartitionSpec as P

WINDOW = 256
NS_ITERS = 5
RATE_ROWS = 16
VMEM_LIMIT = 56 * 1024 * 1024

attn_temp = 5.0
step_size = 0.5
quintic_one = 3.4445
quintic_two = -4.775
quintic_three = 2.0315

f32 = jnp.float32
bf16 = jnp.bfloat16
NN = (((1,), (0,)), ((), ()))
NT = (((1,), (1,)), ((), ()))


def mm(left, right, dims=NN):
    return lax.dot_general(left, right, dims, preferred_element_type=f32)


def split(value):
    high = value.astype(bf16)
    return high, (value - high.astype(f32)).astype(bf16)


def cat(parts, axis):
    return jnp.concatenate(parts, axis=axis)


def mm_exact_left(left, right):
    return mm(cat([left, left], 1), cat(right, 0))


def mm_split(left, right):
    return mm(cat([left[0], left[0], left[1]], 1), cat([right[0], right[1], right[0]], 0))


def unit_scale(rows):
    wide = rows.astype(f32)
    return lax.rsqrt(jnp.sum(wide * wide, axis=-1, keepdims=True) + 1e-06)


def silu_parts(gate_pre):
    sigma = 0.5 * jnp.tanh(0.5 * gate_pre) + 0.5
    return sigma, gate_pre * sigma


def rate_column(packed, token_blocks):
    turned = packed.astype(f32).T
    columns = []
    for at in range(token_blocks):
        parts = [turned[:, at + token_blocks * piece : at + token_blocks * piece + 1] for piece in range(3)]
        columns.append(parts[0] + parts[1] + parts[2])
    return cat(columns, 0)


def split_weights(gate, up, down):
    both = split(cat([gate, up], 1))
    turned = split(down.T)
    return cat(both, 0), cat(turned, 0)


def chunk_grads(key_ref, value_ref, gate_up, down_turned):
    rows = value_ref.shape[0] - RATE_ROWS
    keys = key_ref[:rows]
    values = value_ref[:rows]
    rate = rate_column(key_ref[rows:], rows // 256)
    scale = unit_scale(keys)
    hidden_width = down_turned.shape[1]
    pre = mm(cat([keys, keys], 1), gate_up) * scale
    gate_pre, up_pre = pre[:, :hidden_width], pre[:, hidden_width:]
    sigma, gate_act = silu_parts(gate_pre)
    back = mm(cat([values, values], 1), down_turned) * (rate * scale)
    slope = sigma + gate_act * (1.0 - sigma)
    term_gate = split(back * up_pre * slope)
    term_up = split(back * gate_act)
    term_down = split(gate_act * up_pre * rate)
    key_turned = keys.T
    value_turned = values.T
    key_turned = cat([key_turned, key_turned], 1)
    value_turned = cat([value_turned, value_turned], 1)
    return (
        mm(key_turned, cat(term_gate, 0)),
        mm(key_turned, cat(term_up, 0)),
        mm(value_turned, cat(term_down, 0)),
    )


def gram_of(parts):
    high, low = parts
    return mm(cat([high, high, low], 1), cat([high, low, high], 1), NT)


def orthogonal(grads):
    iterates = []
    for grad in grads:
        norm = jnp.sqrt(jnp.sum(grad * grad, keepdims=True)) + 1e-06
        iterates.append(grad / norm)
    for _ in range(NS_ITERS):
        following = []
        for iterate in iterates:
            parts = split(iterate)
            gram = gram_of(parts)
            gram_parts = split(gram)
            poly = quintic_two * gram + quintic_three * mm_split(gram_parts, gram_parts)
            following.append(quintic_one * iterate + mm_split(split(poly), parts))
        iterates = following
    return iterates


def band(query_rows, key_rows, value_rows, masked):
    query_half = (query_rows.astype(f32) * unit_scale(query_rows)).astype(bf16)
    key_half = (key_rows.astype(f32) * unit_scale(key_rows)).astype(bf16)
    scores = mm(query_half, key_half, NT)
    query_pos = lax.broadcasted_iota(jnp.int32, scores.shape, 0)
    key_pos = lax.broadcasted_iota(jnp.int32, scores.shape, 1)
    distance = query_pos + WINDOW - key_pos
    valid = (distance >= 0) & (distance < WINDOW)
    if masked is not None:
        valid = valid & ((key_pos >= WINDOW) | jnp.logical_not(masked))
    weights = jnp.where(valid, jnp.exp(attn_temp * (scores - 1.0)), 0.0)
    probs = (weights / jnp.sum(weights, axis=-1, keepdims=True)).astype(bf16)
    return mm(probs, value_rows)


def apply_fast(query_rows, gate, up, down, gains):
    scale = unit_scale(query_rows)
    both = split(cat([gate, up], 1))
    pre = mm_exact_left(query_rows, both) * scale
    hidden_width = gate.shape[1]
    gate_pre, up_pre = pre[:, :hidden_width], pre[:, hidden_width:]
    hidden = silu_parts(gate_pre)[1] * up_pre
    fast_out = mm_split(split(hidden), split(down))
    mean_square = jnp.mean(fast_out * fast_out, axis=-1, keepdims=True)
    return fast_out * lax.rsqrt(mean_square + 1e-05) * gains


def pack_kernel(keys_ref, values_ref, rates_ref, key_msg, value_msg):
    rows = keys_ref.shape[0]
    key_msg[:rows] = keys_ref[...]
    key_msg[rows:] = rates_ref[...]
    value_msg[:rows] = values_ref[...]
    value_msg[rows:] = jnp.zeros_like(rates_ref)


def local_band_kernel(queries_ref, keys_ref, values_ref, out_ref):
    groups, rows, _ = queries_ref.shape
    for group in range(groups):
        for at in range(1, rows // WINDOW):
            upper = (at + 1) * WINDOW
            out_ref[group, at * WINDOW - WINDOW : at * WINDOW] = band(
                queries_ref[group, at * WINDOW : upper],
                keys_ref[group, upper - 2 * WINDOW : upper],
                values_ref[group, upper - 2 * WINDOW : upper],
                None,
            )


def accumulate(acc, key_ref, value_ref, gate_up, down_turned):
    for at, part in enumerate(chunk_grads(key_ref, value_ref, gate_up, down_turned)):
        acc[at] = part if acc[at] is None else acc[at] + part


def grads_kernel(chunks, carried, *refs):
    chunk_refs, refs = refs[: 2 * chunks], refs[2 * chunks :]
    gate_ref, up_ref, down_ref = refs[:3]
    out_ref = refs[-1]
    acc = [refs[3][at] for at in range(3)] if carried else [None] * 3
    gate_up, down_turned = split_weights(gate_ref[...], up_ref[...], down_ref[...])
    for at in range(chunks):
        accumulate(acc, chunk_refs[2 * at], chunk_refs[2 * at + 1], gate_up, down_turned)
    for at in range(3):
        out_ref[at] = acc[at]


def update_kernel(
    place_ref,
    last_key, last_value, near_key, near_value, past_key, past_value,
    gate_ref, up_ref, down_ref, acc_ref,
    query_ref, key_ref, value_ref, local_ref, gains_ref,
    *out_refs,
    first_group, keep_weights,
):
    gate, up, down = gate_ref[...], up_ref[...], down_ref[...]
    acc = [acc_ref[at] for at in range(3)]
    gate_up, down_turned = split_weights(gate, up, down)
    accumulate(acc, last_key, last_value, gate_up, down_turned)
    ortho = orthogonal(acc)
    gate = gate + step_size * ortho[0]
    up = up + step_size * ortho[1]
    down = down + step_size * ortho[2].T
    if keep_weights:
        out_refs[1][...] = gate
        out_refs[2][...] = up
        out_refs[3][...] = down
    rows = query_ref.shape[0]
    tail = slice(rows - WINDOW, rows)
    is_first = place_ref[0] == 0
    is_near = place_ref[1] == 1
    halo = []
    for near, last, past in ((near_key, last_key, past_key), (near_value, last_value, past_value)):
        chosen = jnp.where(is_near, near[tail], last[tail])
        if not first_group:
            chosen = jnp.where(is_first, past[tail], chosen)
        halo.append(chosen)
    head_block = band(
        query_ref[:WINDOW],
        cat([halo[0], key_ref[:WINDOW]], 0),
        cat([halo[1], value_ref[:WINDOW]], 0),
        is_first if first_group else None,
    )
    normed = apply_fast(query_ref[...], gate, up, down, gains_ref[...])
    out_refs[0][:WINDOW] = (head_block + normed[:WINDOW]).astype(bf16)
    if rows > WINDOW:
        out_refs[0][WINDOW:] = (local_ref[...] + normed[WINDOW:]).astype(bf16)


def project_kernel(count, order_ref, proj_ref, *refs):
    out_ref = refs[-1]
    total = None
    width = refs[0].shape[1]
    for at in range(count):
        start = pl.multiple_of(order_ref[at] * width, width)
        term = mm(refs[at][...], proj_ref[pl.ds(start, width), :])
        total = term if total is None else total + term
    out_ref[...] = total.astype(out_ref.dtype)


def project_last_kernel(count, order_ref, proj_ref, *refs):
    out_ref = refs[-1]
    project_kernel(count, order_ref, proj_ref, *refs[:count], out_ref.at[out_ref.shape[0] - 1])
    earlier = refs[count]
    for at in range(out_ref.shape[0] - 1):
        out_ref[at] = earlier[at]


VMEM = pl.BlockSpec(memory_space=pltpu.VMEM)
SMEM = pl.BlockSpec(memory_space=pltpu.SMEM)


def call(kernel, out_shape, operands, scalars=0, flops=0, name=None, aliases=None):
    return pl.pallas_call(
        kernel,
        out_shape=out_shape,
        in_specs=[SMEM] * scalars + [VMEM] * (len(operands) - scalars),
        out_specs=jax.tree.map(lambda _: VMEM, out_shape),
        compiler_params=pltpu.CompilerParams(vmem_limit_bytes=VMEM_LIMIT),
        cost_estimate=pl.CostEstimate(flops=flops, bytes_accessed=1 << 20, transcendentals=0),
        input_output_aliases=aliases or {},
        name=name,
    )(*operands)


def shape(dims, dtype):
    return jax.ShapeDtypeStruct(dims, dtype)


def partner(index, step, count):
    return index ^ step if count & (count - 1) == 0 else (index + step) % count


def shifted(value, axis, step):
    count = lax.axis_size(axis)
    return lax.ppermute(value, axis, [(at, partner(at, step, count)) for at in range(count)])


def spread(key_msg, value_msg):
    key_one = shifted(key_msg, "ctx", 1)
    value_one = shifted(value_msg, "ctx", 1)
    key_two = shifted(key_msg, "ctx", 2)
    value_two = shifted(value_msg, "ctx", 2)
    key_three = shifted(key_two, "ctx", 1)
    value_three = shifted(value_one, "ctx", 2)
    return (key_one, value_one), (key_two, value_two), (key_three, value_three)


def body(queries, keys, values, rates, w_gate, w_up, w_down, gains, out_proj):
    groups, rows, width = queries.shape
    hidden = w_gate.shape[2]
    heads = lax.axis_size("head")
    ctx_at = lax.axis_index("ctx")
    head_at = lax.axis_index("head")
    place = jnp.stack([ctx_at, ctx_at % 2]).astype(jnp.int32)
    order = jnp.stack([head_at ^ at for at in range(heads)]).astype(jnp.int32)

    pieces = []
    left = rates[0]
    for _ in range(3):
        piece = lax.reduce_precision(left, 8, 7)
        pieces.append(piece.reshape(groups, rows // 256, 256))
        left = left - piece
    packed = jnp.concatenate(pieces, axis=1)
    packed = jnp.pad(packed, ((0, 0), (0, RATE_ROWS - packed.shape[1]), (0, 0))).astype(bf16)

    gate, up, down = w_gate[0], w_up[0], w_down[0]
    gain_row = gains
    message = shape((rows + RATE_ROWS, width), bf16)
    own = [
        call(pack_kernel, [message, message], [keys[g], values[g], packed[g]], name="pack")
        for g in range(groups)
    ]
    acc_shape = shape((3, width, hidden), f32)
    chunk_flops = 12 * rows * width * hidden * 2

    def grads(chunks, weights, acc):
        operands = [ref for chunk in chunks for ref in chunk] + list(weights)
        if acc is not None:
            operands.append(acc)
        return call(
            functools.partial(grads_kernel, len(chunks), acc is not None),
            acc_shape, operands, flops=chunk_flops * len(chunks), name="grads",
        )

    local = call(
        local_band_kernel,
        shape((groups, rows - WINDOW, width), f32),
        [queries, keys, values],
        flops=groups * rows * WINDOW * width * 8,
        name="local_band",
    )

    proj = lax.all_to_all(
        out_proj.reshape(width, heads, -1).transpose(1, 0, 2), "head", split_axis=0, concat_axis=0
    ).reshape(heads * width, -1)

    gathered = []
    weights = (gate, up, down)
    past = None
    projected = []
    for g in range(groups):
        one, two, three = spread(*own[g])
        acc = grads([own[g]], weights, None)
        acc = grads([one, two], weights, acc)
        last = g == groups - 1
        outs = [shape((rows, width), bf16)]
        if not last:
            outs += [shape(w.shape, f32) for w in weights]
        results = call(
            functools.partial(update_kernel, first_group=g == 0, keep_weights=not last),
            outs,
            [place, *three, *one, *(past or three), *weights, acc,
             queries[g], keys[g], values[g], local[g], gain_row],
            scalars=1,
            flops=chunk_flops + 3 * NS_ITERS * 36 * width ** 3 + 9 * rows * width * hidden * 2,
            name="update",
        )
        combined = results[0]
        weights = tuple(results[1:])
        past = three
        shards = [combined, shifted(combined, "head", 1)]
        for step in range(2, heads, 2):
            other = shifted(combined, "head", step)
            shards += [other, shifted(other, "head", 1)]
        columns = proj.shape[1]
        if not last:
            projected.append(call(
                functools.partial(project_kernel, heads),
                shape((rows, columns), bf16),
                [order, proj, *shards],
                scalars=1, flops=2 * rows * width * heads * columns, name="project",
            ))
        else:
            earlier = jnp.stack(projected)
            output = call(
                functools.partial(project_last_kernel, heads),
                shape((groups, rows, columns), bf16),
                [order, proj, *shards, earlier],
                scalars=1, flops=2 * rows * width * heads * columns, name="project_last",
            )
    return output


def solution(mesh):
    return jax.shard_map(
        body,
        mesh=mesh,
        in_specs=(
            P(None, "ctx", "head"),
            P(None, "ctx", "head"),
            P(None, "ctx", "head"),
            P("head", None, "ctx"),
            P("head", None, None),
            P("head", None, None),
            P("head", None, None),
            P("head", None),
            P("head", None),
        ),
        out_specs=P(None, "ctx", "head"),
        check_vma=False,
    )
```

```python
import functools

import jax
import jax.numpy as jnp
from jax import lax
from jax.experimental import pallas as pl
from jax.experimental.pallas import tpu as pltpu
from jax.sharding import PartitionSpec as P

WINDOW = 256
NS_ITERS = 5
RATE_ROWS = 16
VMEM_LIMIT = 20 * 1024 * 1024
PIECES = 8
UPDATE_FLOPS = 30_000_000_000
MESSAGE_VMEM = 60 * 1024 * 1024

attn_temp = 5.0
step_size = 0.5
quintic_one = 3.4445
quintic_two = -4.775
quintic_three = 2.0315

f32 = jnp.float32
bf16 = jnp.bfloat16
NN = (((1,), (0,)), ((), ()))
NT = (((1,), (1,)), ((), ()))


def mm(left, right, dims=NN):
    return lax.dot_general(left, right, dims, preferred_element_type=f32)


def split(value):
    high = value.astype(bf16)
    return high, (value - high.astype(f32)).astype(bf16)


def cat(parts, axis):
    return jnp.concatenate(parts, axis=axis)


def mm_split(left, right):
    return mm(cat([left[0], left[0], left[1]], 1), cat([right[0], right[1], right[0]], 0))


def unit_scale(rows):
    wide = rows.astype(f32)
    return lax.rsqrt(jnp.sum(wide * wide, axis=-1, keepdims=True) + 1e-06)


def silu_parts(gate_pre):
    sigma = 0.5 * jnp.tanh(0.5 * gate_pre) + 0.5
    return sigma, gate_pre * sigma


def rate_column(packed, token_blocks):
    turned = packed.astype(f32).T
    columns = []
    for at in range(token_blocks):
        parts = [turned[:, at + token_blocks * piece : at + token_blocks * piece + 1] for piece in range(3)]
        columns.append(parts[0] + parts[1] + parts[2])
    return cat(columns, 0)


def stacked_split(value):
    return cat(split(value), 0)


def joined(stacked):
    rows = stacked.shape[0] // 2
    return stacked[:rows].astype(f32) + stacked[rows:].astype(f32)


TOKEN_TILE = 256


def add_chunk(acc, key_ref, value_ref, rate_ref, gate_up_ref, down_turned_ref):
    hidden_width = down_turned_ref.shape[1]
    tiles = value_ref.shape[0] // TOKEN_TILE
    rate = rate_column(rate_ref[...], tiles)
    state = [{} for _ in range(tiles)]

    def forward(at):
        tile = state[at]
        rows = slice(at * TOKEN_TILE, at * TOKEN_TILE + TOKEN_TILE)
        keys, values = key_ref[rows], value_ref[rows]
        tile["rate"], tile["scale"] = rate[rows], unit_scale(keys)
        tile["keys"], tile["values"] = keys.T, values.T
        tile["pre"] = mm(cat([keys, keys], 1), gate_up_ref[...])
        tile["back"] = mm(cat([values, values], 1), down_turned_ref[...])

    def middle(at):
        tile = state[at]
        pre = tile["pre"] * tile["scale"]
        gate_pre, up_pre = pre[:, :hidden_width], pre[:, hidden_width:]
        sigma, gate_act = silu_parts(gate_pre)
        back = tile["back"] * (tile["rate"] * tile["scale"])
        slope = sigma + gate_act * (1.0 - sigma)
        terms = (back * up_pre * slope, back * gate_act, gate_act * up_pre * tile["rate"])
        tile["terms"] = [cat(split(term), 0) for term in terms]

    def backward(at):
        tile = state[at]
        turned = [cat([tile[name]] * 2, 1) for name in ("keys", "keys", "values")]
        for place, (left, right) in enumerate(zip(turned, tile["terms"])):
            part = mm(left, right)
            acc[place] = part if acc[place] is None else acc[place] + part

    for step in range(tiles + 2):
        for lag, stage in enumerate((forward, middle, backward)):
            if 0 <= step - lag < tiles:
                stage(step - lag)


NS_PASSES = (1, 1, 3, 3, 3)


def parts_of(value, passes):
    return (value.astype(bf16),) if passes == 1 else split(value)


def plus_turned(matrix):
    return matrix + matrix.T


def gram_of(parts):
    whole = mm(parts[0], parts[0], NT)
    return whole if len(parts) == 1 else whole + plus_turned(mm(parts[0], parts[1], NT))


def square_of(parts):
    whole = mm(parts[0], parts[0])
    return whole if len(parts) == 1 else whole + plus_turned(mm(parts[0], parts[1]))


def product_of(left, right):
    return mm(left[0], right[0]) if len(left) == 1 else mm_split(left, right)


def orthogonal(grads):
    iterates = [
        grad * (1.0 / (jnp.sqrt(jnp.sum(grad * grad, keepdims=True)) + 1e-06)) for grad in grads
    ]
    for passes in NS_PASSES:
        parts = [parts_of(iterate, passes) for iterate in iterates]
        grams = [gram_of(part) for part in parts]
        squares = [square_of(parts_of(gram, passes)) for gram in grams]
        polys = [quintic_two * gram + quintic_three * square for gram, square in zip(grams, squares)]
        iterates = [
            quintic_one * iterate + product_of(parts_of(poly, passes), part)
            for iterate, poly, part in zip(iterates, polys, parts)
        ]
    return iterates


def band(query_rows, key_rows, value_rows, masked):
    query_half = (query_rows.astype(f32) * unit_scale(query_rows)).astype(bf16)
    key_half = (key_rows.astype(f32) * unit_scale(key_rows)).astype(bf16)
    scores = mm(query_half, key_half, NT)
    query_pos = lax.broadcasted_iota(jnp.int32, scores.shape, 0)
    key_pos = lax.broadcasted_iota(jnp.int32, scores.shape, 1)
    distance = query_pos + WINDOW - key_pos
    valid = (distance >= 0) & (distance < WINDOW)
    if masked is not None:
        valid = valid & ((key_pos >= WINDOW) | jnp.logical_not(masked))
    weights = jnp.where(valid, jnp.exp(attn_temp * (scores - 1.0)), 0.0)
    probs = (weights / jnp.sum(weights, axis=-1, keepdims=True)).astype(bf16)
    return mm(probs, value_rows)


def apply_fast(query_rows, gate_up, down_turned, gains):
    hidden_width = down_turned.shape[1]
    width = down_turned.shape[0] // 2
    pre = mm(cat([query_rows, query_rows], 1), gate_up) * unit_scale(query_rows)
    gate_pre, up_pre = pre[:, :hidden_width], pre[:, hidden_width:]
    high, low = split(silu_parts(gate_pre)[1] * up_pre)
    down_high, down_low = down_turned[:width], down_turned[width:]
    fast_out = mm(cat([high, high, low], 1), cat([down_high, down_low, down_high], 1), NT)
    mean_square = jnp.mean(fast_out * fast_out, axis=-1, keepdims=True)
    return fast_out * lax.rsqrt(mean_square + 1e-05) * gains


def rate_tile(rates_ref, group, blocks):
    left = [rates_ref[0, group : group + 1, at * 256 : at * 256 + 256] for at in range(blocks)]
    row_at = lax.broadcasted_iota(jnp.int32, (RATE_ROWS, 256), 0)
    tile = jnp.zeros((RATE_ROWS, 256), f32)
    for part in range(3):
        for at in range(blocks):
            rounded = left[at].astype(bf16).astype(f32)
            left[at] = left[at] - rounded
            tile = jnp.where(row_at == part * blocks + at, rounded, tile)
    return tile.astype(bf16)


def message_kernel(group, keys_ref, values_ref, rates_ref, out_ref, held, in_sems, out_sems):
    rows = keys_ref.shape[1]
    piece = 2 * rows // PIECES
    spans = [(at * piece, piece) for at in range(PIECES)] + [(2 * rows, RATE_ROWS)]
    outgoing = [
        pltpu.make_async_copy(held.at[pl.ds(*span)], out_ref.at[pl.ds(*span)], out_sems.at[at])
        for at, span in enumerate(spans)
    ]
    incoming = []
    for at, (start, size) in enumerate(spans[:-1]):
        source = keys_ref if start < rows else values_ref
        incoming.append(pltpu.make_async_copy(
            source.at[group, pl.ds(start % rows, size)], held.at[pl.ds(start, size)], in_sems.at[at]
        ))
        incoming[-1].start()
    held[2 * rows :] = rate_tile(rates_ref, group, rows // 256)
    outgoing[-1].start()
    for at in range(PIECES):
        incoming[at].wait()
        outgoing[at].start()
    for copy in outgoing:
        copy.wait()


def later_message_kernel(group, keys_ref, values_ref, rates_ref, out_ref):
    rows = keys_ref.shape[1]
    out_ref[:rows] = keys_ref[group]
    out_ref[rows : 2 * rows] = values_ref[group]
    out_ref[2 * rows :] = rate_tile(rates_ref, group, rows // 256)


def message_parts(message_ref):
    rows = (message_ref.shape[0] - RATE_ROWS) // 2
    return message_ref.at[:rows], message_ref.at[rows : 2 * rows], message_ref.at[2 * rows :]


def local_band_kernel(queries_ref, keys_ref, values_ref, out_ref):
    groups, rows, _ = queries_ref.shape
    for group in range(groups):
        for at in range(1, rows // WINDOW):
            upper = (at + 1) * WINDOW
            out_ref[group, at * WINDOW - WINDOW : at * WINDOW] = band(
                queries_ref[group, at * WINDOW : upper],
                keys_ref[group, upper - 2 * WINDOW : upper],
                values_ref[group, upper - 2 * WINDOW : upper],
                None,
            )


def first_grads_kernel(message, gate_ref, up_ref, down_ref, out_ref, gate_up_ref, down_turned_ref):
    gate_up_ref[...] = stacked_split(cat([gate_ref[...], up_ref[...]], 1))
    down_turned_ref[...] = stacked_split(down_ref[...].T)
    acc = [None] * 3
    add_chunk(acc, *message_parts(message), gate_up_ref, down_turned_ref)
    for at in range(3):
        out_ref[at] = acc[at]


def grads_kernel(chunks, carried, *refs):
    messages, refs = refs[:chunks], refs[chunks:]
    gate_up_ref, down_turned_ref = refs[:2]
    out_ref = refs[-1]
    acc = [refs[2][at] for at in range(3)] if carried else [None] * 3
    for message in messages:
        add_chunk(acc, *message_parts(message), gate_up_ref, down_turned_ref)
    for at in range(3):
        out_ref[at] = acc[at]


def update_kernel(parts, *refs):
    gate_up_ref, down_turned_ref, acc_ref, gate_up_out, down_turned_out, held = refs[parts:]
    message = refs[0]
    if parts > 1:
        message, start = held, 0
        for ref in refs[:parts]:
            held[start : start + ref.shape[0]] = ref[...]
            start += ref.shape[0]
    acc = [acc_ref[at] for at in range(3)]
    add_chunk(acc, *message_parts(message), gate_up_ref, down_turned_ref)
    ortho = orthogonal(acc)
    gate_up_out[...] = stacked_split(joined(gate_up_ref) + step_size * cat(ortho[:2], 1))
    down_turned_out[...] = stacked_split(joined(down_turned_ref) + step_size * ortho[2])


def tails(refs, rows):
    found = []
    for end in (rows, 2 * rows):
        for ref in refs:
            if end <= ref.shape[0]:
                found.append(ref[end - WINDOW : end])
                break
            end = end - ref.shape[0]
    return found


def combine_kernel(group, counts, *refs):
    near, refs = refs[: counts[0]], refs[counts[0] :]
    last, refs = refs[: counts[1]], refs[counts[1] :]
    past, refs = refs[: counts[2]], refs[counts[2] :]
    gate_up_ref, down_turned_ref, queries_ref, keys_ref, values_ref, local_ref, gains_ref, out_ref = refs
    rows = queries_ref.shape[1]
    query_rows = queries_ref.at[group]
    place = lax.axis_index("ctx")
    is_first = place == 0
    is_near = lax.rem(place, 2) == 1
    halo = [jnp.where(is_near, *pair) for pair in zip(tails(near, rows), tails(last, rows))]
    if group > 0:
        halo = [jnp.where(is_first, *pair) for pair in zip(tails(past, rows), halo)]
    head_block = band(
        query_rows[:WINDOW],
        cat([halo[0], keys_ref[group, :WINDOW]], 0),
        cat([halo[1], values_ref[group, :WINDOW]], 0),
        is_first if group == 0 else None,
    )
    normed = apply_fast(query_rows[...], gate_up_ref[...], down_turned_ref[...], gains_ref[...])
    out_ref[:WINDOW] = (head_block + normed[:WINDOW]).astype(bf16)
    if rows > WINDOW:
        out_ref[WINDOW:] = (local_ref[group] + normed[WINDOW:]).astype(bf16)


def pick_kernel(proj_ref, own_ref, other_ref):
    core = lax.rem(lax.axis_index("head"), 2)
    width = proj_ref.shape[0]
    for chip in range(own_ref.shape[1] // width):
        span = slice(chip * width, chip * width + width)
        for side, ref in ((core, own_ref), (1 - core, other_ref)):
            ref[:, span] = proj_ref[:, pl.ds(pl.multiple_of((2 * chip + side) * width, width), width)]


def relay_kernel(one_ref, two_ref, upper_ref, lower_ref):
    rows = upper_ref.shape[0]
    upper_ref[...] = two_ref[:rows]
    lower_ref[...] = one_ref[rows:]


def pair_kernel(own_ref, other_ref, own_proj, other_proj, kept_ref, *sent_refs):
    chip = lax.div(lax.axis_index("head"), 2)
    width = kept_ref.shape[1]
    both = cat([own_ref[...], other_ref[...]], 1)
    for step, ref in enumerate((kept_ref, *sent_refs)):
        span = pl.ds(pl.multiple_of((chip ^ step) * width, width), width)
        ref[...] = mm(both, cat([own_proj[:, span], other_proj[:, span]], 0)).astype(ref.dtype)


def total_of(refs):
    total = refs[0][...]
    for ref in refs[1:]:
        total = total + ref[...].astype(f32)
    return total.astype(bf16)


def finish_kernel(*refs):
    refs[-1][...] = total_of(refs[:-1])


def finish_last_kernel(count, *refs):
    out_ref = refs[-1]
    out_ref[out_ref.shape[0] - 1] = total_of(refs[:count])
    for at, earlier in enumerate(refs[count:-1]):
        out_ref[at] = earlier[...]


VMEM = pl.BlockSpec(memory_space=pltpu.VMEM)
ANYWHERE = pl.BlockSpec(memory_space=pl.ANY)


def call(kernel, out_shape, operands, name, after=(), flops=0, scratch=()):
    count = len(operands)

    def reading(*refs):
        kernel(*refs[:count], *refs[count + len(after) :])

    return pl.pallas_call(
        reading,
        out_shape=out_shape,
        in_specs=[VMEM] * count + [ANYWHERE] * len(after),
        out_specs=jax.tree.map(lambda _: VMEM, out_shape),
        scratch_shapes=scratch,
        compiler_params=pltpu.CompilerParams(vmem_limit_bytes=VMEM_LIMIT),
        cost_estimate=pl.CostEstimate(flops=flops, bytes_accessed=0, transcendentals=0),
        name=name,
    )(*operands, *after)


def shape(dims, dtype):
    return jax.ShapeDtypeStruct(dims, dtype)


def first_message(keys, values, rates):
    _, rows, width = keys.shape
    dims = (2 * rows + RATE_ROWS, width)
    return pl.pallas_call(
        functools.partial(message_kernel, 0),
        out_shape=shape(dims, bf16),
        in_specs=[ANYWHERE, ANYWHERE, VMEM],
        out_specs=ANYWHERE,
        scratch_shapes=[
            pltpu.VMEM(dims, bf16), pltpu.SemaphoreType.DMA((PIECES,)), pltpu.SemaphoreType.DMA((PIECES + 1,)),
        ],
        compiler_params=pltpu.CompilerParams(vmem_limit_bytes=MESSAGE_VMEM),
        cost_estimate=pl.CostEstimate(flops=0, bytes_accessed=0, transcendentals=0),
        name="message",
    )(keys, values, rates)


def later_message(keys, values, rates, group, after):
    _, rows, width = keys.shape
    return call(
        functools.partial(later_message_kernel, group), shape((2 * rows + RATE_ROWS, width), bf16),
        [keys, values, rates], "message", after,
    )


def shifted(value, axis, step):
    count = lax.axis_size(axis)
    return lax.ppermute(value, axis, [(at, at ^ step) for at in range(count)])


def partial_sums(combined, own_proj, other_proj, after):
    rows, width = combined.shape
    chips = lax.axis_size("head") // 2
    kept, *sent = call(
        pair_kernel, [shape((rows, width), f32)] + [shape((rows, width), bf16)] * (chips - 1),
        [combined, shifted(combined, "head", 1), own_proj, other_proj], "pair", after,
    )
    return [kept] + [shifted(block, "head", 2 * step) for step, block in enumerate(sent, 1)]


def opposite(one, two, after):
    rows, width = one.shape
    half = rows // 2 // 16 * 16
    upper, lower = call(
        relay_kernel, [shape((half, width), bf16), shape((rows - half, width), bf16)], [one, two], "relay", after
    )
    return shifted(upper, "ctx", 1), shifted(lower, "ctx", 2)


def body(queries, keys, values, rates, w_gate, w_up, w_down, gains, out_proj):
    groups, rows, width = queries.shape
    hidden = w_gate.shape[2]
    chips = lax.axis_size("head") // 2
    acc_shape = shape((3, width, hidden), f32)
    weight_shapes = [shape((2 * width, 2 * hidden), bf16), shape((2 * width, hidden), bf16)]
    picked = shape((width, out_proj.shape[1] // 2), bf16)

    message = first_message(keys, values, rates)
    one, two = shifted(message, "ctx", 1), shifted(message, "ctx", 2)
    acc, *weights = call(
        first_grads_kernel, [acc_shape, *weight_shapes], [message, w_gate[0], w_up[0], w_down[0]], "grads"
    )
    own_proj, for_other = call(pick_kernel, [picked, picked], [out_proj], "pick", [acc])
    other_proj = shifted(for_other, "head", 1)
    local = call(
        local_band_kernel, shape((groups, rows - WINDOW, width), f32), [queries, keys, values],
        "local_band", [own_proj],
    )
    last = past = opposite(one, two, [local])

    totals = []
    combined = None
    for g in range(groups):
        if g > 0:
            acc = call(
                functools.partial(grads_kernel, 1, False), acc_shape, [message, *weights], "grads", [combined]
            )
            totals.append(partial_sums(combined, own_proj, other_proj, [acc]))
        acc = call(
            functools.partial(grads_kernel, 2, True), acc_shape, [one, two, *weights, acc], "grads",
            [local] if g == 0 else totals[-1][:1],
        )
        near, after = one, []
        if g < groups - 1:
            message = later_message(keys, values, rates, g + 1, [acc])
            one, two, three = (shifted(message, "ctx", step) for step in (1, 2, 3))
            after = [message]
        weights = call(
            functools.partial(update_kernel, len(last)), weight_shapes, [*last, *weights, acc], "update", after,
            flops=UPDATE_FLOPS if g < groups - 1 else 0, scratch=[pltpu.VMEM(message.shape, bf16)],
        )
        combined = call(
            functools.partial(combine_kernel, g, (1, len(last), len(past))),
            shape((rows, width), bf16),
            [near, *last, *past, *weights, queries, keys, values, local, gains],
            "combine",
        )
        past, last = last, [three]
    finished = [
        call(finish_kernel, shape((rows, width), bf16), total, "finish", [combined]) for total in totals
    ]
    total = partial_sums(combined, own_proj, other_proj, finished)
    return call(
        functools.partial(finish_last_kernel, len(total)), shape((groups, rows, width), bf16),
        [*total, *finished], "finish_last",
    )


def solution(mesh):
    return jax.shard_map(
        body,
        mesh=mesh,
        in_specs=(
            P(None, "ctx", "head"),
            P(None, "ctx", "head"),
            P(None, "ctx", "head"),
            P("head", None, "ctx"),
            P("head", None, None),
            P("head", None, None),
            P("head", None, None),
            P("head", None),
            P("head", None),
        ),
        out_specs=P(None, "ctx", "head"),
        check_vma=False,
    )
```

```python
import functools

import jax
import jax.numpy as jnp
from jax import lax
from jax.experimental import pallas as pl
from jax.experimental.pallas import tpu as pltpu
from jax.sharding import PartitionSpec as P

WINDOW = 256
NS_ITERS = 5
RATE_ROWS = 16
VMEM_LIMIT = 20 * 1024 * 1024
PIECES = 8
UPDATE_FLOPS = 30_000_000_000
MESSAGE_VMEM = 60 * 1024 * 1024

attn_temp = 5.0
step_size = 0.5
quintic_one = 3.4445
quintic_two = -4.775
quintic_three = 2.0315

f32 = jnp.float32
bf16 = jnp.bfloat16
NN = (((1,), (0,)), ((), ()))
NT = (((1,), (1,)), ((), ()))


def mm(left, right, dims=NN):
    return lax.dot_general(left, right, dims, preferred_element_type=f32)


def split(value):
    high = value.astype(bf16)
    return high, (value - high.astype(f32)).astype(bf16)


def cat(parts, axis):
    return jnp.concatenate(parts, axis=axis)


def mm_split(left, right):
    return mm(cat([left[0], left[0], left[1]], 1), cat([right[0], right[1], right[0]], 0))


def unit_scale(rows):
    wide = rows.astype(f32)
    return lax.rsqrt(jnp.sum(wide * wide, axis=-1, keepdims=True) + 1e-06)


def silu_parts(gate_pre):
    sigma = 0.5 * jnp.tanh(0.5 * gate_pre) + 0.5
    return sigma, gate_pre * sigma


def rate_column(packed, token_blocks):
    turned = packed.astype(f32).T
    columns = []
    for at in range(token_blocks):
        parts = [turned[:, at + token_blocks * piece : at + token_blocks * piece + 1] for piece in range(3)]
        columns.append(parts[0] + parts[1] + parts[2])
    return cat(columns, 0)


def stacked_split(value):
    return cat(split(value), 0)


def joined(stacked):
    rows = stacked.shape[0] // 2
    return stacked[:rows].astype(f32) + stacked[rows:].astype(f32)


TOKEN_TILE = 256


def add_chunk(acc, key_ref, value_ref, rate_ref, gate_up_ref, down_turned_ref):
    hidden_width = down_turned_ref.shape[1]
    tiles = value_ref.shape[0] // TOKEN_TILE
    rate = rate_column(rate_ref[...], tiles)
    state = [{} for _ in range(tiles)]

    def forward(at):
        tile = state[at]
        rows = slice(at * TOKEN_TILE, at * TOKEN_TILE + TOKEN_TILE)
        keys, values = key_ref[rows], value_ref[rows]
        tile["rate"], tile["scale"] = rate[rows], unit_scale(keys)
        tile["keys"], tile["values"] = keys.T, values.T
        tile["pre"] = mm(cat([keys, keys], 1), gate_up_ref[...])
        tile["back"] = mm(cat([values, values], 1), down_turned_ref[...])

    def middle(at):
        tile = state[at]
        pre = tile["pre"] * tile["scale"]
        gate_pre, up_pre = pre[:, :hidden_width], pre[:, hidden_width:]
        sigma, gate_act = silu_parts(gate_pre)
        back = tile["back"] * (tile["rate"] * tile["scale"])
        slope = sigma + gate_act * (1.0 - sigma)
        terms = (back * up_pre * slope, back * gate_act, gate_act * up_pre * tile["rate"])
        tile["terms"] = [cat(split(term), 0) for term in terms]

    def backward(at):
        tile = state[at]
        turned = [cat([tile[name]] * 2, 1) for name in ("keys", "keys", "values")]
        for place, (left, right) in enumerate(zip(turned, tile["terms"])):
            part = mm(left, right)
            acc[place] = part if acc[place] is None else acc[place] + part

    for step in range(tiles + 2):
        for lag, stage in enumerate((forward, middle, backward)):
            if 0 <= step - lag < tiles:
                stage(step - lag)


NS_PASSES = (1, 1, 3, 3, 3)


def parts_of(value, passes):
    return (value.astype(bf16),) if passes == 1 else split(value)


def plus_turned(matrix):
    return matrix + matrix.T


def gram_of(parts):
    whole = mm(parts[0], parts[0], NT)
    return whole if len(parts) == 1 else whole + plus_turned(mm(parts[0], parts[1], NT))


def square_of(parts):
    whole = mm(parts[0], parts[0])
    return whole if len(parts) == 1 else whole + plus_turned(mm(parts[0], parts[1]))


def product_of(left, right):
    return mm(left[0], right[0]) if len(left) == 1 else mm_split(left, right)


def orthogonal(grads):
    iterates = [
        grad * (1.0 / (jnp.sqrt(jnp.sum(grad * grad, keepdims=True)) + 1e-06)) for grad in grads
    ]
    for passes in NS_PASSES:
        parts = [parts_of(iterate, passes) for iterate in iterates]
        grams = [gram_of(part) for part in parts]
        squares = [square_of(parts_of(gram, passes)) for gram in grams]
        polys = [quintic_two * gram + quintic_three * square for gram, square in zip(grams, squares)]
        iterates = [
            quintic_one * iterate + product_of(parts_of(poly, passes), part)
            for iterate, poly, part in zip(iterates, polys, parts)
        ]
    return iterates


def band(query_rows, key_rows, value_rows, masked):
    query_half = (query_rows.astype(f32) * unit_scale(query_rows)).astype(bf16)
    key_half = (key_rows.astype(f32) * unit_scale(key_rows)).astype(bf16)
    scores = mm(query_half, key_half, NT)
    query_pos = lax.broadcasted_iota(jnp.int32, scores.shape, 0)
    key_pos = lax.broadcasted_iota(jnp.int32, scores.shape, 1)
    distance = query_pos + WINDOW - key_pos
    valid = (distance >= 0) & (distance < WINDOW)
    if masked is not None:
        valid = valid & ((key_pos >= WINDOW) | jnp.logical_not(masked))
    weights = jnp.where(valid, jnp.exp(attn_temp * (scores - 1.0)), 0.0)
    probs = (weights / jnp.sum(weights, axis=-1, keepdims=True)).astype(bf16)
    return mm(probs, value_rows)


def apply_fast(query_rows, gate_up, down_turned, gains):
    hidden_width = down_turned.shape[1]
    width = down_turned.shape[0] // 2
    pre = mm(cat([query_rows, query_rows], 1), gate_up) * unit_scale(query_rows)
    gate_pre, up_pre = pre[:, :hidden_width], pre[:, hidden_width:]
    high, low = split(silu_parts(gate_pre)[1] * up_pre)
    down_high, down_low = down_turned[:width], down_turned[width:]
    fast_out = mm(cat([high, high, low], 1), cat([down_high, down_low, down_high], 1), NT)
    mean_square = jnp.mean(fast_out * fast_out, axis=-1, keepdims=True)
    return fast_out * lax.rsqrt(mean_square + 1e-05) * gains


def rate_tile(rates_ref, group, blocks):
    left = [rates_ref[0, group : group + 1, at * 256 : at * 256 + 256] for at in range(blocks)]
    row_at = lax.broadcasted_iota(jnp.int32, (RATE_ROWS, 256), 0)
    tile = jnp.zeros((RATE_ROWS, 256), f32)
    for part in range(3):
        for at in range(blocks):
            rounded = left[at].astype(bf16).astype(f32)
            left[at] = left[at] - rounded
            tile = jnp.where(row_at == part * blocks + at, rounded, tile)
    return tile.astype(bf16)


def message_kernel(group, keys_ref, values_ref, rates_ref, out_ref, sems):
    rows = keys_ref.shape[1]
    piece = 2 * rows // PIECES
    copies = []
    for at in range(PIECES):
        start = at * piece
        source = keys_ref if start < rows else values_ref
        copies.append(pltpu.make_async_copy(
            source.at[group, pl.ds(start % rows, piece)], out_ref.at[pl.ds(start, piece)], sems.at[at]
        ))
        copies[-1].start()
    out_ref[2 * rows :] = rate_tile(rates_ref, group, rows // 256)
    for copy in copies:
        copy.wait()


def later_message_kernel(group, keys_ref, values_ref, rates_ref, out_ref):
    rows = keys_ref.shape[1]
    out_ref[:rows] = keys_ref[group]
    out_ref[rows : 2 * rows] = values_ref[group]
    out_ref[2 * rows :] = rate_tile(rates_ref, group, rows // 256)


def message_parts(message_ref):
    rows = (message_ref.shape[0] - RATE_ROWS) // 2
    return message_ref.at[:rows], message_ref.at[rows : 2 * rows], message_ref.at[2 * rows :]


def local_band_kernel(queries_ref, keys_ref, values_ref, out_ref):
    groups, rows, _ = queries_ref.shape
    for group in range(groups):
        for at in range(1, rows // WINDOW):
            upper = (at + 1) * WINDOW
            out_ref[group, at * WINDOW - WINDOW : at * WINDOW] = band(
                queries_ref[group, at * WINDOW : upper],
                keys_ref[group, upper - 2 * WINDOW : upper],
                values_ref[group, upper - 2 * WINDOW : upper],
                None,
            )


def first_grads_kernel(message, gate_ref, up_ref, down_ref, out_ref, gate_up_ref, down_turned_ref):
    gate_up_ref[...] = stacked_split(cat([gate_ref[...], up_ref[...]], 1))
    down_turned_ref[...] = stacked_split(down_ref[...].T)
    acc = [None] * 3
    add_chunk(acc, *message_parts(message), gate_up_ref, down_turned_ref)
    for at in range(3):
        out_ref[at] = acc[at]


def grads_kernel(chunks, carried, *refs):
    messages, refs = refs[:chunks], refs[chunks:]
    gate_up_ref, down_turned_ref = refs[:2]
    out_ref = refs[-1]
    acc = [refs[2][at] for at in range(3)] if carried else [None] * 3
    for message in messages:
        add_chunk(acc, *message_parts(message), gate_up_ref, down_turned_ref)
    for at in range(3):
        out_ref[at] = acc[at]


def last_grads_kernel(parts, *refs):
    gate_up_ref, down_turned_ref, acc_ref, out_ref, held = refs[parts:]
    start = 0
    for ref in refs[:parts]:
        held[start : start + ref.shape[0]] = ref[...]
        start += ref.shape[0]
    acc = [acc_ref[at] for at in range(3)]
    add_chunk(acc, *message_parts(held), gate_up_ref, down_turned_ref)
    for at in range(3):
        out_ref[at] = acc[at]


def tails(refs, rows):
    found = []
    for end in (rows, 2 * rows):
        for ref in refs:
            if end <= ref.shape[0]:
                found.append(ref[end - WINDOW : end])
                break
            end = end - ref.shape[0]
    return found


def update_kernel(group, counts, *refs):
    near, refs = refs[: counts[0]], refs[counts[0] :]
    last, refs = refs[: counts[1]], refs[counts[1] :]
    past, refs = refs[: counts[2]], refs[counts[2] :]
    gate_up_ref, down_turned_ref, acc_ref, queries_ref, keys_ref, values_ref, local_ref, gains_ref, *refs = refs
    out_ref, gate_up_out, down_turned_out = refs
    ortho = orthogonal([acc_ref[at] for at in range(3)])
    gate_up_out[...] = stacked_split(joined(gate_up_ref) + step_size * cat(ortho[:2], 1))
    down_turned_out[...] = stacked_split(joined(down_turned_ref) + step_size * ortho[2])
    rows = queries_ref.shape[1]
    query_rows = queries_ref.at[group]
    place = lax.axis_index("ctx")
    is_first = place == 0
    is_near = lax.rem(place, 2) == 1
    halo = [jnp.where(is_near, *pair) for pair in zip(tails(near, rows), tails(last, rows))]
    if group > 0:
        halo = [jnp.where(is_first, *pair) for pair in zip(tails(past, rows), halo)]
    head_block = band(
        query_rows[:WINDOW],
        cat([halo[0], keys_ref[group, :WINDOW]], 0),
        cat([halo[1], values_ref[group, :WINDOW]], 0),
        is_first if group == 0 else None,
    )
    normed = apply_fast(query_rows[...], gate_up_out[...], down_turned_out[...], gains_ref[...])
    out_ref[:WINDOW] = (head_block + normed[:WINDOW]).astype(bf16)
    if rows > WINDOW:
        out_ref[WINDOW:] = (local_ref[group] + normed[WINDOW:]).astype(bf16)


def pick_kernel(proj_ref, own_ref, other_ref):
    core = lax.rem(lax.axis_index("head"), 2)
    width = proj_ref.shape[0]
    for chip in range(own_ref.shape[1] // width):
        span = slice(chip * width, chip * width + width)
        for side, ref in ((core, own_ref), (1 - core, other_ref)):
            ref[:, span] = proj_ref[:, pl.ds(pl.multiple_of((2 * chip + side) * width, width), width)]


def relay_kernel(one_ref, two_ref, upper_ref, lower_ref):
    rows = upper_ref.shape[0]
    upper_ref[...] = two_ref[:rows]
    lower_ref[...] = one_ref[rows:]


def pair_kernel(own_ref, other_ref, own_proj, other_proj, kept_ref, *sent_refs):
    chip = lax.div(lax.axis_index("head"), 2)
    width = kept_ref.shape[1]
    both = cat([own_ref[...], other_ref[...]], 1)
    for step, ref in enumerate((kept_ref, *sent_refs)):
        span = pl.ds(pl.multiple_of((chip ^ step) * width, width), width)
        ref[...] = mm(both, cat([own_proj[:, span], other_proj[:, span]], 0)).astype(ref.dtype)


def own_part_kernel(own_ref, own_proj, *out_refs):
    chip = lax.div(lax.axis_index("head"), 2)
    width = own_ref.shape[1]
    for step, ref in enumerate(out_refs):
        span = pl.ds(pl.multiple_of((chip ^ step) * width, width), width)
        ref[...] = mm(own_ref[...], own_proj[:, span])


def other_part_kernel(chips, other_ref, other_proj, *refs):
    chip = lax.div(lax.axis_index("head"), 2)
    width = other_ref.shape[1]
    for step in range(chips):
        span = pl.ds(pl.multiple_of((chip ^ step) * width, width), width)
        ref = refs[chips + step]
        ref[...] = (refs[step][...] + mm(other_ref[...], other_proj[:, span])).astype(ref.dtype)


def total_of(refs):
    total = refs[0][...]
    for ref in refs[1:]:
        total = total + ref[...].astype(f32)
    return total.astype(bf16)


def add_kernel(count, *refs):
    for at in range(count):
        ref = refs[2 * count + at]
        ref[...] = (refs[at][...] + refs[count + at][...].astype(f32)).astype(ref.dtype)


def finish_kernel(*refs):
    refs[-1][...] = total_of(refs[:-1])


def finish_last_kernel(count, *refs):
    out_ref = refs[-1]
    out_ref[out_ref.shape[0] - 1] = total_of(refs[:count])
    for at, earlier in enumerate(refs[count:-1]):
        out_ref[at] = earlier[...]


VMEM = pl.BlockSpec(memory_space=pltpu.VMEM)
ANYWHERE = pl.BlockSpec(memory_space=pl.ANY)


def call(kernel, out_shape, operands, name, after=(), flops=0, scratch=()):
    count = len(operands)

    def reading(*refs):
        kernel(*refs[:count], *refs[count + len(after) :])

    return pl.pallas_call(
        reading,
        out_shape=out_shape,
        in_specs=[VMEM] * count + [ANYWHERE] * len(after),
        out_specs=jax.tree.map(lambda _: VMEM, out_shape),
        scratch_shapes=scratch,
        compiler_params=pltpu.CompilerParams(vmem_limit_bytes=VMEM_LIMIT),
        cost_estimate=pl.CostEstimate(flops=flops, bytes_accessed=0, transcendentals=0),
        name=name,
    )(*operands, *after)


def shape(dims, dtype):
    return jax.ShapeDtypeStruct(dims, dtype)


def first_message(keys, values, rates):
    _, rows, width = keys.shape
    dims = (2 * rows + RATE_ROWS, width)
    return pl.pallas_call(
        functools.partial(message_kernel, 0),
        out_shape=shape(dims, bf16),
        in_specs=[ANYWHERE, ANYWHERE, VMEM],
        out_specs=VMEM,
        scratch_shapes=[pltpu.SemaphoreType.DMA((PIECES,))],
        compiler_params=pltpu.CompilerParams(vmem_limit_bytes=MESSAGE_VMEM),
        cost_estimate=pl.CostEstimate(flops=0, bytes_accessed=0, transcendentals=0),
        name="message",
    )(keys, values, rates)


def later_message(keys, values, rates, group, after):
    _, rows, width = keys.shape
    return call(
        functools.partial(later_message_kernel, group), shape((2 * rows + RATE_ROWS, width), bf16),
        [keys, values, rates], "message", after,
    )


def shifted(value, axis, step):
    count = lax.axis_size(axis)
    return lax.ppermute(value, axis, [(at, at ^ step) for at in range(count)])


def pair(combined, own_proj, other_proj, types, after=()):
    rows, width = combined.shape
    return call(
        pair_kernel, [shape((rows, width), kind) for kind in types],
        [combined, shifted(combined, "head", 1), own_proj, other_proj], "pair", after,
    )


def to_chip(block, step):
    return shifted(block, "head", 2 * step)


def direct_sums(combined, own_proj, other_proj):
    chips = lax.axis_size("head") // 2
    rows, width = combined.shape
    other = shifted(combined, "head", 1)
    parts = call(
        own_part_kernel, [shape((rows, width), f32)] * chips, [combined, own_proj], "own_part",
        flops=UPDATE_FLOPS,
    )
    kept, *sent = call(
        functools.partial(other_part_kernel, chips),
        [shape((rows, width), f32)] + [shape((rows, width), bf16)] * (chips - 1),
        [other, other_proj, *parts], "other_part",
    )
    return [kept] + [to_chip(block, step) for step, block in enumerate(sent, 1)]


class HalvingSums:
    def __init__(self, combined, own_proj, other_proj, after):
        self.chips = lax.axis_size("head") // 2
        types = [bf16 if at % 2 else f32 for at in range(self.chips)]
        self.held = dict(enumerate(pair(combined, own_proj, other_proj, types, after)))
        self.terms = [self.held.pop(0)]
        self.marker = self.terms[0]
        self.pass_on(1)

    def pass_on(self, step):
        self.step = step
        sent = sorted((at for at in self.held if at & step), reverse=True)
        came = {at ^ step: to_chip(self.held.pop(at), step) for at in sent}
        self.terms.append(came.pop(0))
        self.came = came

    def next_step(self, after):
        step = 2 * self.step
        order = sorted(self.held)
        sums = call(
            functools.partial(add_kernel, len(order)),
            [shape(self.held[at].shape, bf16 if at & step else f32) for at in order],
            [self.held[at] for at in order] + [self.came[at] for at in order], "add", after,
        )
        self.held = dict(zip(order, sums))
        self.marker = sums[0]
        self.pass_on(step)


def opposite(one, two, after):
    rows, width = one.shape
    half = rows // 2 // 16 * 16
    upper, lower = call(
        relay_kernel, [shape((half, width), bf16), shape((rows - half, width), bf16)], [one, two], "relay", after
    )
    return shifted(upper, "ctx", 1), shifted(lower, "ctx", 2)


def body(queries, keys, values, rates, w_gate, w_up, w_down, gains, out_proj):
    groups, rows, width = queries.shape
    hidden = w_gate.shape[2]
    chips = lax.axis_size("head") // 2
    acc_shape = shape((3, width, hidden), f32)
    weight_shapes = [shape((2 * width, 2 * hidden), bf16), shape((2 * width, hidden), bf16)]
    picked = shape((width, out_proj.shape[1] // 2), bf16)

    message = first_message(keys, values, rates)
    one, two = shifted(message, "ctx", 1), shifted(message, "ctx", 2)
    acc, *weights = call(
        first_grads_kernel, [acc_shape, *weight_shapes], [message, w_gate[0], w_up[0], w_down[0]], "grads"
    )
    own_proj, for_other = call(pick_kernel, [picked, picked], [out_proj], "pick", [acc])
    other_proj = shifted(for_other, "head", 1)
    local = call(
        local_band_kernel, shape((groups, rows - WINDOW, width), f32), [queries, keys, values],
        "local_band", [own_proj],
    )
    last = past = opposite(one, two, [local])

    totals = []
    combined = None
    for g in range(groups):
        if g > 0:
            acc = call(
                functools.partial(grads_kernel, 1, False), acc_shape, [message, *weights], "grads", [combined]
            )
            last = opposite(one, two, [acc])
            totals.append(HalvingSums(combined, own_proj, other_proj, [acc]))
        acc = call(
            functools.partial(grads_kernel, 2, True), acc_shape, [one, two, *weights, acc], "grads",
            [local] if g == 0 else [totals[-1].marker],
        )
        near, after = one, []
        if g < groups - 1:
            message = later_message(keys, values, rates, g + 1, [acc])
            one, two = shifted(message, "ctx", 1), shifted(message, "ctx", 2)
            after = [message]
        acc = call(
            functools.partial(last_grads_kernel, len(last)), acc_shape, [*last, *weights, acc], "grads", after,
            scratch=[pltpu.VMEM(message.shape, bf16)],
        )
        after = [acc]
        while g > 0 and totals[-1].held:
            totals[-1].next_step(after)
            after = [totals[-1].marker]
        combined, *weights = call(
            functools.partial(update_kernel, g, (1, len(last), len(past))),
            [shape((rows, width), bf16), *weight_shapes],
            [near, *last, *past, *weights, acc, queries, keys, values, local, gains],
            "update", after, flops=UPDATE_FLOPS if g < groups - 1 else 0,
        )
        past = last
    total = direct_sums(combined, own_proj, other_proj)
    finished = [
        call(finish_kernel, shape((rows, width), bf16), earlier.terms, "finish", total[:1]) for earlier in totals
    ]
    return call(
        functools.partial(finish_last_kernel, len(total)), shape((groups, rows, width), bf16),
        [*total, *finished], "finish_last",
    )


def solution(mesh):
    return jax.shard_map(
        body,
        mesh=mesh,
        in_specs=(
            P(None, "ctx", "head"),
            P(None, "ctx", "head"),
            P(None, "ctx", "head"),
            P("head", None, "ctx"),
            P("head", None, None),
            P("head", None, None),
            P("head", None, None),
            P("head", None),
            P("head", None),
        ),
        out_specs=P(None, "ctx", "head"),
        check_vma=False,
    )
```

```python
import functools

import jax
import jax.numpy as jnp
from jax import lax
from jax.experimental import pallas as pl
from jax.experimental.pallas import tpu as pltpu
from jax.sharding import PartitionSpec as P

WINDOW = 256
NS_ITERS = 5
RATE_ROWS = 16
VMEM_LIMIT = 20 * 1024 * 1024
UPDATE_FLOPS = 30_000_000_000
MESSAGE_VMEM = 60 * 1024 * 1024

attn_temp = 5.0
step_size = 0.5
quintic_one = 3.4445
quintic_two = -4.775
quintic_three = 2.0315

f32 = jnp.float32
bf16 = jnp.bfloat16
NN = (((1,), (0,)), ((), ()))
NT = (((1,), (1,)), ((), ()))


def mm(left, right, dims=NN):
    return lax.dot_general(left, right, dims, preferred_element_type=f32)


def split(value):
    high = value.astype(bf16)
    return high, (value - high.astype(f32)).astype(bf16)


def cat(parts, axis):
    return jnp.concatenate(parts, axis=axis)


def mm_split(left, right):
    return mm(cat([left[0], left[0], left[1]], 1), cat([right[0], right[1], right[0]], 0))


def unit_scale(rows):
    wide = rows.astype(f32)
    return lax.rsqrt(jnp.sum(wide * wide, axis=-1, keepdims=True) + 1e-06)


def silu_parts(gate_pre):
    sigma = 0.5 * jnp.tanh(0.5 * gate_pre) + 0.5
    return sigma, gate_pre * sigma


def rate_column(packed, token_blocks):
    turned = packed.astype(f32).T
    columns = []
    for at in range(token_blocks):
        parts = [turned[:, at + token_blocks * piece : at + token_blocks * piece + 1] for piece in range(3)]
        columns.append(parts[0] + parts[1] + parts[2])
    return cat(columns, 0)


def stacked_split(value):
    return cat(split(value), 0)


def joined(stacked):
    rows = stacked.shape[0] // 2
    return stacked[:rows].astype(f32) + stacked[rows:].astype(f32)


TOKEN_TILE = 256


def add_messages(acc, messages, gate_up_ref, down_turned_ref):
    hidden_width = down_turned_ref.shape[1]
    block = min(256, hidden_width)
    blocks = [slice(at, at + block) for at in range(0, hidden_width, block)]
    sums = [[None if part is None else part[:, span] for span in blocks] for part in acc]
    tiles = []
    for message in messages:
        key_ref, value_ref, rate_ref = message_parts(message)
        count = value_ref.shape[0] // TOKEN_TILE
        rate = rate_column(rate_ref[...], count)
        for at in range(count):
            tiles.append((key_ref, value_ref, rate, slice(at * TOKEN_TILE, at * TOKEN_TILE + TOKEN_TILE)))
    state = [{} for _ in tiles]

    def forward(at):
        key_ref, value_ref, rate, rows = tiles[at]
        tile = state[at]
        keys, values = key_ref[rows], value_ref[rows]
        tile["rate"], tile["scale"] = rate[rows], unit_scale(keys)
        both_keys, both_values = cat([keys, keys], 1), cat([values, values], 1)
        tile["pre"] = []
        for span in blocks:
            gate_pre = mm(both_keys, gate_up_ref[:, span])
            yield
            up_pre = mm(both_keys, gate_up_ref[:, hidden_width + span.start : hidden_width + span.stop])
            yield
            tile["pre"].append((gate_pre, up_pre, mm(both_values, down_turned_ref[:, span])))
            yield
        tile["turned"] = [part.T for part in (keys, keys, values)]
        yield

    def middle(at):
        tile = state[at]
        tile["terms"] = []
        for gate_pre, up_pre, back in tile["pre"]:
            gate_pre, up_pre = gate_pre * tile["scale"], up_pre * tile["scale"]
            sigma, gate_act = silu_parts(gate_pre)
            back = back * (tile["rate"] * tile["scale"])
            slope = sigma + gate_act * (1.0 - sigma)
            terms = (back * up_pre * slope, back * gate_act, gate_act * up_pre * tile["rate"])
            tile["terms"].append([term.astype(bf16) for term in terms])
            yield

    def backward(at):
        tile = state[at]
        for column, terms in enumerate(tile["terms"]):
            for place, (left, right) in enumerate(zip(tile["turned"], terms)):
                part, before = mm(left, right), sums[place][column]
                sums[place][column] = part if before is None else before + part
                yield

    for step in range(len(tiles) + 2):
        stages = [
            stage(step - lag)
            for lag, stage in ((2, backward), (1, middle), (0, forward))
            if 0 <= step - lag < len(tiles)
        ]
        while stages:
            stages = [stage for stage in stages if next(stage, True) is None]
    for place in range(3):
        acc[place] = cat(sums[place], 1)


NS_PASSES = (1, 1, 3, 3, 3)


def parts_of(value, passes):
    return (value.astype(bf16),) if passes == 1 else split(value)


def plus_turned(matrix):
    return matrix + matrix.T


def gram_of(parts):
    whole = mm(parts[0], parts[0], NT)
    return whole if len(parts) == 1 else whole + plus_turned(mm(parts[0], parts[1], NT))


def square_of(parts):
    whole = mm(parts[0], parts[0])
    return whole if len(parts) == 1 else whole + plus_turned(mm(parts[0], parts[1]))


def product_of(left, right):
    return mm(left[0], right[0]) if len(left) == 1 else mm_split(left, right)


def orthogonal(grads):
    iterates = [
        grad * (1.0 / (jnp.sqrt(jnp.sum(grad * grad, keepdims=True)) + 1e-06)) for grad in grads
    ]
    for passes in NS_PASSES:
        parts = [parts_of(iterate, passes) for iterate in iterates]
        grams = [gram_of(part) for part in parts]
        squares = [square_of(parts_of(gram, passes)) for gram in grams]
        polys = [quintic_two * gram + quintic_three * square for gram, square in zip(grams, squares)]
        iterates = [
            quintic_one * iterate + product_of(parts_of(poly, passes), part)
            for iterate, poly, part in zip(iterates, polys, parts)
        ]
    return iterates


def band(query_rows, key_rows, value_rows, masked):
    query_half = (query_rows.astype(f32) * unit_scale(query_rows)).astype(bf16)
    key_half = (key_rows.astype(f32) * unit_scale(key_rows)).astype(bf16)
    scores = mm(query_half, key_half, NT)
    query_pos = lax.broadcasted_iota(jnp.int32, scores.shape, 0)
    key_pos = lax.broadcasted_iota(jnp.int32, scores.shape, 1)
    distance = query_pos + WINDOW - key_pos
    valid = (distance >= 0) & (distance < WINDOW)
    if masked is not None:
        valid = valid & ((key_pos >= WINDOW) | jnp.logical_not(masked))
    weights = jnp.where(valid, jnp.exp(attn_temp * (scores - 1.0)), 0.0)
    probs = (weights / jnp.sum(weights, axis=-1, keepdims=True)).astype(bf16)
    return mm(probs, value_rows)


def apply_fast(query_rows, gate_up, down_turned, gains):
    hidden_width = down_turned.shape[1]
    width = down_turned.shape[0] // 2
    pre = mm(cat([query_rows, query_rows], 1), gate_up) * unit_scale(query_rows)
    gate_pre, up_pre = pre[:, :hidden_width], pre[:, hidden_width:]
    high, low = split(silu_parts(gate_pre)[1] * up_pre)
    down_high, down_low = down_turned[:width], down_turned[width:]
    fast_out = mm(cat([high, high, low], 1), cat([down_high, down_low, down_high], 1), NT)
    mean_square = jnp.mean(fast_out * fast_out, axis=-1, keepdims=True)
    return fast_out * lax.rsqrt(mean_square + 1e-05) * gains


def rate_tile(rates_ref, group, blocks):
    left = [rates_ref[0, group : group + 1, at * 256 : at * 256 + 256] for at in range(blocks)]
    row_at = lax.broadcasted_iota(jnp.int32, (RATE_ROWS, 256), 0)
    tile = jnp.zeros((RATE_ROWS, 256), f32)
    for part in range(3):
        for at in range(blocks):
            rounded = left[at].astype(bf16).astype(f32)
            left[at] = left[at] - rounded
            tile = jnp.where(row_at == part * blocks + at, rounded, tile)
    return tile.astype(bf16)


def message_kernel(group, keys_ref, values_ref, rates_ref, out_ref):
    rows = keys_ref.shape[0]
    out_ref[:rows] = keys_ref[...]
    out_ref[rows : 2 * rows] = values_ref[...]
    out_ref[2 * rows :] = rate_tile(rates_ref, group, rows // 256)


def later_message_kernel(group, keys_ref, values_ref, rates_ref, out_ref):
    rows = keys_ref.shape[1]
    out_ref[:rows] = keys_ref[group]
    out_ref[rows : 2 * rows] = values_ref[group]
    out_ref[2 * rows :] = rate_tile(rates_ref, group, rows // 256)


def message_parts(message_ref):
    rows = (message_ref.shape[0] - RATE_ROWS) // 2
    return message_ref.at[:rows], message_ref.at[rows : 2 * rows], message_ref.at[2 * rows :]


def local_band_kernel(queries_ref, keys_ref, values_ref, out_ref):
    groups, rows, _ = queries_ref.shape
    for group in range(groups):
        for at in range(1, rows // WINDOW):
            upper = (at + 1) * WINDOW
            out_ref[group, at * WINDOW - WINDOW : at * WINDOW] = band(
                queries_ref[group, at * WINDOW : upper],
                keys_ref[group, upper - 2 * WINDOW : upper],
                values_ref[group, upper - 2 * WINDOW : upper],
                None,
            )


def first_grads_kernel(message, gate_ref, up_ref, down_ref, out_ref, gate_up_ref, down_turned_ref):
    gate_up_ref[...] = stacked_split(cat([gate_ref[...], up_ref[...]], 1))
    down_turned_ref[...] = stacked_split(down_ref[...].T)
    acc = [None] * 3
    add_messages(acc, [message], gate_up_ref, down_turned_ref)
    for at in range(3):
        out_ref[at] = acc[at]


def grads_kernel(chunks, carried, *refs):
    messages, refs = refs[:chunks], refs[chunks:]
    gate_up_ref, down_turned_ref = refs[:2]
    out_ref = refs[-1]
    acc = [refs[2][at] for at in range(3)] if carried else [None] * 3
    add_messages(acc, messages, gate_up_ref, down_turned_ref)
    for at in range(3):
        out_ref[at] = acc[at]


def last_grads_kernel(parts, *refs):
    gate_up_ref, down_turned_ref, acc_ref, out_ref, held = refs[parts:]
    start = 0
    for ref in refs[:parts]:
        held[start : start + ref.shape[0]] = ref[...]
        start += ref.shape[0]
    acc = [acc_ref[at] for at in range(3)]
    add_messages(acc, [held], gate_up_ref, down_turned_ref)
    for at in range(3):
        out_ref[at] = acc[at]


def tails(refs, rows):
    found = []
    for end in (rows, 2 * rows):
        for ref in refs:
            if end <= ref.shape[0]:
                found.append(ref[end - WINDOW : end])
                break
            end = end - ref.shape[0]
    return found


def update_kernel(group, counts, *refs):
    near, refs = refs[: counts[0]], refs[counts[0] :]
    last, refs = refs[: counts[1]], refs[counts[1] :]
    past, refs = refs[: counts[2]], refs[counts[2] :]
    gate_up_ref, down_turned_ref, acc_ref, queries_ref, keys_ref, values_ref, local_ref, gains_ref, *refs = refs
    out_ref, gate_up_out, down_turned_out = refs
    ortho = orthogonal([acc_ref[at] for at in range(3)])
    gate_up_out[...] = stacked_split(joined(gate_up_ref) + step_size * cat(ortho[:2], 1))
    down_turned_out[...] = stacked_split(joined(down_turned_ref) + step_size * ortho[2])
    rows = queries_ref.shape[1]
    query_rows = queries_ref.at[group]
    place = lax.axis_index("ctx")
    is_first = place == 0
    is_near = lax.rem(place, 2) == 1
    halo = [jnp.where(is_near, *pair) for pair in zip(tails(near, rows), tails(last, rows))]
    if group > 0:
        halo = [jnp.where(is_first, *pair) for pair in zip(tails(past, rows), halo)]
    head_block = band(
        query_rows[:WINDOW],
        cat([halo[0], keys_ref[group, :WINDOW]], 0),
        cat([halo[1], values_ref[group, :WINDOW]], 0),
        is_first if group == 0 else None,
    )
    normed = apply_fast(query_rows[...], gate_up_out[...], down_turned_out[...], gains_ref[...])
    out_ref[:WINDOW] = (head_block + normed[:WINDOW]).astype(bf16)
    if rows > WINDOW:
        out_ref[WINDOW:] = (local_ref[group] + normed[WINDOW:]).astype(bf16)


def pick_kernel(proj_ref, own_ref, other_ref):
    core = lax.rem(lax.axis_index("head"), 2)
    width = proj_ref.shape[0]
    for chip in range(own_ref.shape[1] // width):
        span = slice(chip * width, chip * width + width)
        for side, ref in ((core, own_ref), (1 - core, other_ref)):
            ref[:, span] = proj_ref[:, pl.ds(pl.multiple_of((2 * chip + side) * width, width), width)]


def relay_kernel(one_ref, two_ref, upper_ref, lower_ref):
    rows = upper_ref.shape[0]
    upper_ref[...] = two_ref[:rows]
    lower_ref[...] = one_ref[rows:]


def pair_kernel(own_ref, other_ref, own_proj, other_proj, kept_ref, *sent_refs):
    chip = lax.div(lax.axis_index("head"), 2)
    width = kept_ref.shape[1]
    both = cat([own_ref[...], other_ref[...]], 1)
    for step, ref in enumerate((kept_ref, *sent_refs)):
        span = pl.ds(pl.multiple_of((chip ^ step) * width, width), width)
        ref[...] = mm(both, cat([own_proj[:, span], other_proj[:, span]], 0)).astype(ref.dtype)


def own_part_kernel(own_ref, own_proj, *out_refs):
    chip = lax.div(lax.axis_index("head"), 2)
    width = own_ref.shape[1]
    for step, ref in enumerate(out_refs):
        span = pl.ds(pl.multiple_of((chip ^ step) * width, width), width)
        ref[...] = mm(own_ref[...], own_proj[:, span])


def other_part_kernel(chips, other_ref, other_proj, *refs):
    chip = lax.div(lax.axis_index("head"), 2)
    width = other_ref.shape[1]
    for step in range(chips):
        span = pl.ds(pl.multiple_of((chip ^ step) * width, width), width)
        ref = refs[chips + step]
        ref[...] = (refs[step][...] + mm(other_ref[...], other_proj[:, span])).astype(ref.dtype)


def total_of(refs):
    total = refs[0][...]
    for ref in refs[1:]:
        total = total + ref[...].astype(f32)
    return total.astype(bf16)


def add_kernel(count, *refs):
    for at in range(count):
        ref = refs[2 * count + at]
        ref[...] = (refs[at][...] + refs[count + at][...].astype(f32)).astype(ref.dtype)


def finish_kernel(*refs):
    refs[-1][...] = total_of(refs[:-1])


def finish_last_kernel(count, *refs):
    out_ref = refs[-1]
    out_ref[out_ref.shape[0] - 1] = total_of(refs[:count])
    for at, earlier in enumerate(refs[count:-1]):
        out_ref[at] = earlier[...]


VMEM = pl.BlockSpec(memory_space=pltpu.VMEM)
ANYWHERE = pl.BlockSpec(memory_space=pl.ANY)


def call(kernel, out_shape, operands, name, after=(), flops=0, scratch=()):
    count = len(operands)

    def reading(*refs):
        kernel(*refs[:count], *refs[count + len(after) :])

    return pl.pallas_call(
        reading,
        out_shape=out_shape,
        in_specs=[VMEM] * count + [ANYWHERE] * len(after),
        out_specs=jax.tree.map(lambda _: VMEM, out_shape),
        scratch_shapes=scratch,
        compiler_params=pltpu.CompilerParams(vmem_limit_bytes=VMEM_LIMIT),
        cost_estimate=pl.CostEstimate(flops=flops, bytes_accessed=0, transcendentals=0),
        name=name,
    )(*operands, *after)


def shape(dims, dtype):
    return jax.ShapeDtypeStruct(dims, dtype)


def first_message(keys, values, rates):
    _, rows, width = keys.shape
    dims = (2 * rows + RATE_ROWS, width)
    block = pl.BlockSpec((None, rows, width), lambda step: (0, 0, 0))
    return pl.pallas_call(
        functools.partial(message_kernel, 0),
        out_shape=shape(dims, bf16),
        grid=(1,),
        in_specs=[block, block, pl.BlockSpec(rates.shape, lambda step: (0, 0, 0))],
        out_specs=pl.BlockSpec(dims, lambda step: (0, 0)),
        compiler_params=pltpu.CompilerParams(vmem_limit_bytes=MESSAGE_VMEM),
        cost_estimate=pl.CostEstimate(flops=0, bytes_accessed=0, transcendentals=0),
        name="message",
    )(keys, values, rates)


def later_message(keys, values, rates, group, after):
    _, rows, width = keys.shape
    return call(
        functools.partial(later_message_kernel, group), shape((2 * rows + RATE_ROWS, width), bf16),
        [keys, values, rates], "message", after,
    )


def shifted(value, axis, step):
    count = lax.axis_size(axis)
    return lax.ppermute(value, axis, [(at, at ^ step) for at in range(count)])


def pair(combined, own_proj, other_proj, types, after=()):
    rows, width = combined.shape
    return call(
        pair_kernel, [shape((rows, width), kind) for kind in types],
        [combined, shifted(combined, "head", 1), own_proj, other_proj], "pair", after,
    )


def to_chip(block, step):
    return shifted(block, "head", 2 * step)


def direct_sums(combined, own_proj, other_proj):
    chips = lax.axis_size("head") // 2
    rows, width = combined.shape
    other = shifted(combined, "head", 1)
    parts = call(
        own_part_kernel, [shape((rows, width), f32)] * chips, [combined, own_proj], "own_part",
        flops=UPDATE_FLOPS,
    )
    kept, *sent = call(
        functools.partial(other_part_kernel, chips),
        [shape((rows, width), f32)] + [shape((rows, width), bf16)] * (chips - 1),
        [other, other_proj, *parts], "other_part",
    )
    order = [*range(2, chips), 1]
    return [kept] + [to_chip(sent[step - 1], step) for step in order]


class HalvingSums:
    def __init__(self, combined, own_proj, other_proj, after):
        self.chips = lax.axis_size("head") // 2
        types = [bf16 if at % 2 else f32 for at in range(self.chips)]
        self.held = dict(enumerate(pair(combined, own_proj, other_proj, types, after)))
        self.terms = [self.held.pop(0)]
        self.marker = self.terms[0]
        self.pass_on(1)

    def pass_on(self, step):
        self.step = step
        sent = sorted((at for at in self.held if at & step), reverse=True)
        came = {at ^ step: to_chip(self.held.pop(at), step) for at in sent}
        self.terms.append(came.pop(0))
        self.came = came

    def next_step(self, after):
        step = 2 * self.step
        order = sorted(self.held)
        sums = call(
            functools.partial(add_kernel, len(order)),
            [shape(self.held[at].shape, bf16 if at & step else f32) for at in order],
            [self.held[at] for at in order] + [self.came[at] for at in order], "add", after,
        )
        self.held = dict(zip(order, sums))
        self.marker = sums[0]
        self.pass_on(step)


def opposite(one, two, after):
    rows, width = one.shape
    half = rows // 2 // 16 * 16
    upper, lower = call(
        relay_kernel, [shape((half, width), bf16), shape((rows - half, width), bf16)], [one, two], "relay", after
    )
    return shifted(upper, "ctx", 1), shifted(lower, "ctx", 2)


def body(queries, keys, values, rates, w_gate, w_up, w_down, gains, out_proj):
    groups, rows, width = queries.shape
    hidden = w_gate.shape[2]
    chips = lax.axis_size("head") // 2
    acc_shape = shape((3, width, hidden), f32)
    weight_shapes = [shape((2 * width, 2 * hidden), bf16), shape((2 * width, hidden), bf16)]
    picked = shape((width, out_proj.shape[1] // 2), bf16)

    message = first_message(keys, values, rates)
    one, two = shifted(message, "ctx", 1), shifted(message, "ctx", 2)
    acc, *weights = call(
        first_grads_kernel, [acc_shape, *weight_shapes], [message, w_gate[0], w_up[0], w_down[0]], "grads"
    )
    own_proj, for_other = call(pick_kernel, [picked, picked], [out_proj], "pick", [acc])
    other_proj = shifted(for_other, "head", 1)
    local = call(
        local_band_kernel, shape((groups, rows - WINDOW, width), f32), [queries, keys, values],
        "local_band", [own_proj],
    )
    last = past = opposite(one, two, [local])

    totals = []
    combined = None
    for g in range(groups):
        if g > 0:
            acc = call(
                functools.partial(grads_kernel, 1, False), acc_shape, [message, *weights], "grads", [combined]
            )
            totals.append(HalvingSums(combined, own_proj, other_proj, [acc]))
            last = opposite(one, two, [totals[-1].marker])
        acc = call(
            functools.partial(grads_kernel, 2, True), acc_shape, [one, two, *weights, acc], "grads",
            [local] if g == 0 else [totals[-1].marker],
        )
        near, after = one, []
        if g < groups - 1:
            message = later_message(keys, values, rates, g + 1, [acc])
            one, two = shifted(message, "ctx", 1), shifted(message, "ctx", 2)
            after = [message]
        acc = call(
            functools.partial(last_grads_kernel, len(last)), acc_shape, [*last, *weights, acc], "grads", after,
            scratch=[pltpu.VMEM(message.shape, bf16)],
        )
        after = [acc]
        while g > 0 and totals[-1].held:
            totals[-1].next_step(after)
            after = [totals[-1].marker]
        combined, *weights = call(
            functools.partial(update_kernel, g, (1, len(last), len(past))),
            [shape((rows, width), bf16), *weight_shapes],
            [near, *last, *past, *weights, acc, queries, keys, values, local, gains],
            "update", after, flops=UPDATE_FLOPS if g < groups - 1 else 0,
        )
        past = last
    total = direct_sums(combined, own_proj, other_proj)
    finished = [
        call(finish_kernel, shape((rows, width), bf16), earlier.terms, "finish", total[:1]) for earlier in totals
    ]
    return call(
        functools.partial(finish_last_kernel, len(total)), shape((groups, rows, width), bf16),
        [*total, *finished], "finish_last",
    )


def solution(mesh):
    return jax.shard_map(
        body,
        mesh=mesh,
        in_specs=(
            P(None, "ctx", "head"),
            P(None, "ctx", "head"),
            P(None, "ctx", "head"),
            P("head", None, "ctx"),
            P("head", None, None),
            P("head", None, None),
            P("head", None, None),
            P("head", None),
            P("head", None),
        ),
        out_specs=P(None, "ctx", "head"),
        check_vma=False,
    )
```

```python
import functools

import jax
import jax.numpy as jnp
from jax import lax
from jax.experimental import pallas as pl
from jax.experimental.pallas import tpu as pltpu
from jax.sharding import PartitionSpec as P

WINDOW = 256
NS_ITERS = 5
RATE_ROWS = 16
VMEM_LIMIT = 20 * 1024 * 1024
UPDATE_FLOPS = 30_000_000_000
LAST_PIECES = 4
MESSAGE_VMEM = 60 * 1024 * 1024

attn_temp = 5.0
step_size = 0.5
quintic_one = 3.4445
quintic_two = -4.775
quintic_three = 2.0315

f32 = jnp.float32
bf16 = jnp.bfloat16
NN = (((1,), (0,)), ((), ()))
NT = (((1,), (1,)), ((), ()))


def mm(left, right, dims=NN):
    return lax.dot_general(left, right, dims, preferred_element_type=f32)


def split(value):
    high = value.astype(bf16)
    return high, (value - high.astype(f32)).astype(bf16)


def cat(parts, axis):
    return jnp.concatenate(parts, axis=axis)


def mm_split(left, right):
    return mm(cat([left[0], left[0], left[1]], 1), cat([right[0], right[1], right[0]], 0))


def unit_scale(rows):
    wide = rows.astype(f32)
    return lax.rsqrt(jnp.sum(wide * wide, axis=-1, keepdims=True) + 1e-06)


def silu_parts(gate_pre):
    sigma = 0.5 * jnp.tanh(0.5 * gate_pre) + 0.5
    return sigma, gate_pre * sigma


def rate_column(packed, token_blocks):
    turned = packed.astype(f32).T
    columns = []
    for at in range(token_blocks):
        parts = [turned[:, at + token_blocks * piece : at + token_blocks * piece + 1] for piece in range(3)]
        columns.append(parts[0] + parts[1] + parts[2])
    return cat(columns, 0)


def stacked_split(value):
    return cat(split(value), 0)


def joined(stacked):
    rows = stacked.shape[0] // 2
    return stacked[:rows].astype(f32) + stacked[rows:].astype(f32)


TOKEN_TILE = 256


def add_messages(acc, messages, gate_up_ref, down_turned_ref):
    hidden_width = down_turned_ref.shape[1]
    block = min(256, hidden_width)
    blocks = [slice(at, at + block) for at in range(0, hidden_width, block)]
    sums = [[None if part is None else part[:, span] for span in blocks] for part in acc]
    tiles = []
    for message in messages:
        key_ref, value_ref, rate_ref = message_parts(message)
        count = value_ref.shape[0] // TOKEN_TILE
        rate = rate_column(rate_ref[...], count)
        for at in range(count):
            tiles.append((key_ref, value_ref, rate, slice(at * TOKEN_TILE, at * TOKEN_TILE + TOKEN_TILE)))
    state = [{} for _ in tiles]

    def forward(at):
        key_ref, value_ref, rate, rows = tiles[at]
        tile = state[at]
        keys, values = key_ref[rows], value_ref[rows]
        tile["rate"], tile["scale"] = rate[rows], unit_scale(keys)
        both_keys, both_values = cat([keys, keys], 1), cat([values, values], 1)
        tile["pre"] = []
        for span in blocks:
            gate_pre = mm(both_keys, gate_up_ref[:, span])
            yield
            up_pre = mm(both_keys, gate_up_ref[:, hidden_width + span.start : hidden_width + span.stop])
            yield
            tile["pre"].append((gate_pre, up_pre, mm(both_values, down_turned_ref[:, span])))
            yield
        tile["turned"] = [part.T for part in (keys, keys, values)]
        yield

    def middle(at):
        tile = state[at]
        tile["terms"] = []
        for gate_pre, up_pre, back in tile["pre"]:
            gate_pre, up_pre = gate_pre * tile["scale"], up_pre * tile["scale"]
            sigma, gate_act = silu_parts(gate_pre)
            back = back * (tile["rate"] * tile["scale"])
            slope = sigma + gate_act * (1.0 - sigma)
            terms = (back * up_pre * slope, back * gate_act, gate_act * up_pre * tile["rate"])
            tile["terms"].append([term.astype(bf16) for term in terms])
            yield

    def backward(at):
        tile = state[at]
        for column, terms in enumerate(tile["terms"]):
            for place, (left, right) in enumerate(zip(tile["turned"], terms)):
                part, before = mm(left, right), sums[place][column]
                sums[place][column] = part if before is None else before + part
                yield

    for step in range(len(tiles) + 2):
        stages = [
            stage(step - lag)
            for lag, stage in ((2, backward), (1, middle), (0, forward))
            if 0 <= step - lag < len(tiles)
        ]
        while stages:
            stages = [stage for stage in stages if next(stage, True) is None]
    for place in range(3):
        acc[place] = cat(sums[place], 1)


NS_PASSES = (1, 1, 3, 3, 3)


def parts_of(value, passes):
    return (value.astype(bf16),) if passes == 1 else split(value)


def plus_turned(matrix):
    return matrix + matrix.T


def gram_of(parts):
    whole = mm(parts[0], parts[0], NT)
    return whole if len(parts) == 1 else whole + plus_turned(mm(parts[0], parts[1], NT))


def square_of(parts):
    whole = mm(parts[0], parts[0])
    return whole if len(parts) == 1 else whole + plus_turned(mm(parts[0], parts[1]))


def product_of(left, right):
    return mm(left[0], right[0]) if len(left) == 1 else mm_split(left, right)


def orthogonal(grads, beside):
    iterates = [
        grad * (1.0 / (jnp.sqrt(jnp.sum(grad * grad, keepdims=True)) + 1e-06)) for grad in grads
    ]
    for passes in NS_PASSES:
        parts = [parts_of(iterate, passes) for iterate in iterates]
        grams = [gram_of(part) for part in parts]
        if passes > 1 and beside is not None:
            beside()
            beside = None
        squares = [square_of(parts_of(gram, passes)) for gram in grams]
        polys = [quintic_two * gram + quintic_three * square for gram, square in zip(grams, squares)]
        iterates = [
            quintic_one * iterate + product_of(parts_of(poly, passes), part)
            for iterate, poly, part in zip(iterates, polys, parts)
        ]
    return iterates


def band(query_rows, key_rows, value_rows, masked):
    query_half = (query_rows.astype(f32) * unit_scale(query_rows)).astype(bf16)
    key_half = (key_rows.astype(f32) * unit_scale(key_rows)).astype(bf16)
    scores = mm(query_half, key_half, NT)
    query_pos = lax.broadcasted_iota(jnp.int32, scores.shape, 0)
    key_pos = lax.broadcasted_iota(jnp.int32, scores.shape, 1)
    distance = query_pos + WINDOW - key_pos
    valid = (distance >= 0) & (distance < WINDOW)
    if masked is not None:
        valid = valid & ((key_pos >= WINDOW) | jnp.logical_not(masked))
    weights = jnp.where(valid, jnp.exp(attn_temp * (scores - 1.0)), 0.0)
    probs = (weights / jnp.sum(weights, axis=-1, keepdims=True)).astype(bf16)
    return mm(probs, value_rows)


def apply_fast(query_rows, gate_up, down_turned, gains):
    hidden_width = down_turned.shape[1]
    width = down_turned.shape[0] // 2
    pre = mm(cat([query_rows, query_rows], 1), gate_up) * unit_scale(query_rows)
    gate_pre, up_pre = pre[:, :hidden_width], pre[:, hidden_width:]
    high, low = split(silu_parts(gate_pre)[1] * up_pre)
    down_high, down_low = down_turned[:width], down_turned[width:]
    fast_out = mm(cat([high, high, low], 1), cat([down_high, down_low, down_high], 1), NT)
    mean_square = jnp.mean(fast_out * fast_out, axis=-1, keepdims=True)
    return fast_out * lax.rsqrt(mean_square + 1e-05) * gains


def rate_tile(rates_ref, group, blocks):
    left = [rates_ref[0, group : group + 1, at * 256 : at * 256 + 256] for at in range(blocks)]
    row_at = lax.broadcasted_iota(jnp.int32, (RATE_ROWS, 256), 0)
    tile = jnp.zeros((RATE_ROWS, 256), f32)
    for part in range(3):
        for at in range(blocks):
            rounded = left[at].astype(bf16).astype(f32)
            left[at] = left[at] - rounded
            tile = jnp.where(row_at == part * blocks + at, rounded, tile)
    return tile.astype(bf16)


def message_kernel(group, keys_ref, values_ref, rates_ref, out_ref):
    rows = keys_ref.shape[0]
    out_ref[:rows] = keys_ref[...]
    out_ref[rows : 2 * rows] = values_ref[...]
    out_ref[2 * rows :] = rate_tile(rates_ref, group, rows // 256)


def later_message_kernel(group, keys_ref, values_ref, rates_ref, out_ref):
    rows = keys_ref.shape[1]
    out_ref[:rows] = keys_ref[group]
    out_ref[rows : 2 * rows] = values_ref[group]
    out_ref[2 * rows :] = rate_tile(rates_ref, group, rows // 256)


def message_parts(message_ref):
    rows = (message_ref.shape[0] - RATE_ROWS) // 2
    return message_ref.at[:rows], message_ref.at[rows : 2 * rows], message_ref.at[2 * rows :]


def local_band_kernel(queries_ref, keys_ref, values_ref, out_ref):
    groups, rows, _ = queries_ref.shape
    for group in range(groups):
        for at in range(1, rows // WINDOW):
            upper = (at + 1) * WINDOW
            out_ref[group, at * WINDOW - WINDOW : at * WINDOW] = band(
                queries_ref[group, at * WINDOW : upper],
                keys_ref[group, upper - 2 * WINDOW : upper],
                values_ref[group, upper - 2 * WINDOW : upper],
                None,
            )


def first_grads_kernel(message, gate_ref, up_ref, down_ref, out_ref, gate_up_ref, down_turned_ref):
    gate_up_ref[...] = stacked_split(cat([gate_ref[...], up_ref[...]], 1))
    down_turned_ref[...] = stacked_split(down_ref[...].T)
    acc = [None] * 3
    add_messages(acc, [message], gate_up_ref, down_turned_ref)
    for at in range(3):
        out_ref[at] = acc[at]


def grads_kernel(chunks, carried, *refs):
    messages, refs = refs[:chunks], refs[chunks:]
    gate_up_ref, down_turned_ref = refs[:2]
    out_ref = refs[-1]
    acc = [refs[2][at] for at in range(3)] if carried else [None] * 3
    add_messages(acc, messages, gate_up_ref, down_turned_ref)
    for at in range(3):
        out_ref[at] = acc[at]


def last_grads_kernel(parts, *refs):
    gate_up_ref, down_turned_ref, acc_ref, out_ref, held = refs[parts:]
    start = 0
    for ref in reversed(refs[:parts]):
        held[start : start + ref.shape[0]] = ref[...]
        start += ref.shape[0]
    acc = [acc_ref[at] for at in range(3)]
    add_messages(acc, [held], gate_up_ref, down_turned_ref)
    for at in range(3):
        out_ref[at] = acc[at]


def tails(refs, rows):
    found = []
    for end in (rows, 2 * rows):
        for ref in reversed(refs):
            if end <= ref.shape[0]:
                found.append(ref[end - WINDOW : end])
                break
            end = end - ref.shape[0]
    return found


def update_kernel(group, counts, *refs):
    near, refs = refs[: counts[0]], refs[counts[0] :]
    last, refs = refs[: counts[1]], refs[counts[1] :]
    past, refs = refs[: counts[2]], refs[counts[2] :]
    gate_up_ref, down_turned_ref, acc_ref, queries_ref, keys_ref, values_ref, local_ref, gains_ref, *refs = refs
    out_ref, gate_up_out, down_turned_out = refs
    rows = queries_ref.shape[1]
    query_rows = queries_ref.at[group]
    place = lax.axis_index("ctx")
    is_first = place == 0
    is_near = lax.rem(place, 2) == 1
    halo = [jnp.where(is_near, *pair) for pair in zip(tails(near, rows), tails(last, rows))]
    if group > 0:
        halo = [jnp.where(is_first, *pair) for pair in zip(tails(past, rows), halo)]
    head_block = []

    def attend():
        head_block.append(band(
            query_rows[:WINDOW],
            cat([halo[0], keys_ref[group, :WINDOW]], 0),
            cat([halo[1], values_ref[group, :WINDOW]], 0),
            is_first if group == 0 else None,
        ))

    ortho = orthogonal([acc_ref[at] for at in range(3)], attend)
    gate_up_out[...] = stacked_split(joined(gate_up_ref) + step_size * cat(ortho[:2], 1))
    down_turned_out[...] = stacked_split(joined(down_turned_ref) + step_size * ortho[2])
    normed = apply_fast(query_rows[...], gate_up_out[...], down_turned_out[...], gains_ref[...])
    out_ref[:WINDOW] = (head_block[0] + normed[:WINDOW]).astype(bf16)
    if rows > WINDOW:
        out_ref[WINDOW:] = (local_ref[group] + normed[WINDOW:]).astype(bf16)


def pick_kernel(proj_ref, own_ref, other_ref):
    core = lax.rem(lax.axis_index("head"), 2)
    width = proj_ref.shape[0]
    for chip in range(own_ref.shape[1] // width):
        span = slice(chip * width, chip * width + width)
        for side, ref in ((core, own_ref), (1 - core, other_ref)):
            ref[:, span] = proj_ref[:, pl.ds(pl.multiple_of((2 * chip + side) * width, width), width)]


def relay_kernel(start, message_ref, part_ref):
    part_ref[...] = message_ref[start : start + part_ref.shape[0]]


def pair_kernel(own_ref, other_ref, own_proj, other_proj, kept_ref, *sent_refs):
    chip = lax.div(lax.axis_index("head"), 2)
    width = kept_ref.shape[1]
    both = cat([own_ref[...], other_ref[...]], 1)
    for step, ref in enumerate((kept_ref, *sent_refs)):
        span = pl.ds(pl.multiple_of((chip ^ step) * width, width), width)
        ref[...] = mm(both, cat([own_proj[:, span], other_proj[:, span]], 0)).astype(ref.dtype)


def own_part_kernel(own_ref, own_proj, *out_refs):
    chip = lax.div(lax.axis_index("head"), 2)
    width = own_ref.shape[1]
    for step, ref in enumerate(out_refs):
        span = pl.ds(pl.multiple_of((chip ^ step) * width, width), width)
        ref[...] = mm(own_ref[...], own_proj[:, span])


def other_part_kernel(chips, other_ref, other_proj, *refs):
    chip = lax.div(lax.axis_index("head"), 2)
    width = other_ref.shape[1]
    for step in range(chips):
        span = pl.ds(pl.multiple_of((chip ^ step) * width, width), width)
        ref = refs[chips + step]
        ref[...] = (refs[step][...] + mm(other_ref[...], other_proj[:, span])).astype(ref.dtype)


def total_of(refs):
    total = refs[0][...]
    for ref in refs[1:]:
        total = total + ref[...].astype(f32)
    return total.astype(bf16)


def add_kernel(count, *refs):
    for at in range(count):
        ref = refs[2 * count + at]
        ref[...] = (refs[at][...] + refs[count + at][...].astype(f32)).astype(ref.dtype)


def finish_kernel(*refs):
    refs[-1][...] = total_of(refs[:-1])


def finish_last_kernel(count, *refs):
    out_ref, held, sems = refs[-3:]
    terms, earlier = refs[:count], refs[count:-3]
    last = out_ref.shape[0] - 1
    copies = [
        pltpu.make_async_copy(ref, out_ref.at[at], sems.at[at]) for at, ref in enumerate(earlier)
    ]
    piece = held.shape[0] // LAST_PIECES
    for copy in copies:
        copy.start()
    for at in range(LAST_PIECES):
        rows = pl.ds(at * piece, piece)
        held[rows] = total_of([term.at[rows] for term in terms])
        copies.append(pltpu.make_async_copy(held.at[rows], out_ref.at[last, rows], sems.at[last + at]))
        copies[-1].start()
    for copy in copies:
        copy.wait()


VMEM = pl.BlockSpec(memory_space=pltpu.VMEM)
ANYWHERE = pl.BlockSpec(memory_space=pl.ANY)


def call(kernel, out_shape, operands, name, after=(), flops=0, scratch=(), out=VMEM):
    count = len(operands)

    def reading(*refs):
        kernel(*refs[:count], *refs[count + len(after) :])

    return pl.pallas_call(
        reading,
        out_shape=out_shape,
        in_specs=[VMEM] * count + [ANYWHERE] * len(after),
        out_specs=jax.tree.map(lambda _: out, out_shape),
        scratch_shapes=scratch,
        compiler_params=pltpu.CompilerParams(vmem_limit_bytes=VMEM_LIMIT),
        cost_estimate=pl.CostEstimate(flops=flops, bytes_accessed=0, transcendentals=0),
        name=name,
    )(*operands, *after)


def shape(dims, dtype):
    return jax.ShapeDtypeStruct(dims, dtype)


def first_message(keys, values, rates):
    _, rows, width = keys.shape
    dims = (2 * rows + RATE_ROWS, width)
    block = pl.BlockSpec((None, rows, width), lambda step: (0, 0, 0))
    return pl.pallas_call(
        functools.partial(message_kernel, 0),
        out_shape=shape(dims, bf16),
        grid=(1,),
        in_specs=[block, block, pl.BlockSpec(rates.shape, lambda step: (0, 0, 0))],
        out_specs=pl.BlockSpec(dims, lambda step: (0, 0)),
        compiler_params=pltpu.CompilerParams(vmem_limit_bytes=MESSAGE_VMEM),
        cost_estimate=pl.CostEstimate(flops=0, bytes_accessed=0, transcendentals=0),
        name="message",
    )(keys, values, rates)


def later_message(keys, values, rates, group, after):
    _, rows, width = keys.shape
    return call(
        functools.partial(later_message_kernel, group), shape((2 * rows + RATE_ROWS, width), bf16),
        [keys, values, rates], "message", after,
    )


def shifted(value, axis, step):
    count = lax.axis_size(axis)
    return lax.ppermute(value, axis, [(at, at ^ step) for at in range(count)])


def pair(combined, own_proj, other_proj, types, after=()):
    rows, width = combined.shape
    return call(
        pair_kernel, [shape((rows, width), kind) for kind in types],
        [combined, shifted(combined, "head", 1), own_proj, other_proj], "pair", after,
    )


def to_chip(block, step):
    return shifted(block, "head", 2 * step)


def direct_sums(combined, own_proj, other_proj):
    chips = lax.axis_size("head") // 2
    rows, width = combined.shape
    other = shifted(combined, "head", 1)
    parts = call(
        own_part_kernel, [shape((rows, width), f32)] * chips, [combined, own_proj], "own_part",
        flops=UPDATE_FLOPS,
    )
    kept, *sent = call(
        functools.partial(other_part_kernel, chips),
        [shape((rows, width), f32)] + [shape((rows, width), bf16)] * (chips - 1),
        [other, other_proj, *parts], "other_part",
    )
    order = [*range(2, chips), 1]
    return [kept] + [to_chip(sent[step - 1], step) for step in order]


class HalvingSums:
    def __init__(self, combined, own_proj, other_proj, after):
        self.chips = lax.axis_size("head") // 2
        types = [bf16 if at % 2 else f32 for at in range(self.chips)]
        self.held = dict(enumerate(pair(combined, own_proj, other_proj, types, after)))
        self.terms = [self.held.pop(0)]
        self.marker = self.terms[0]
        self.pass_on(1)

    def pass_on(self, step):
        self.step = step
        sent = sorted((at for at in self.held if at & step), reverse=True)
        came = {at ^ step: to_chip(self.held.pop(at), step) for at in sent}
        self.terms.append(came.pop(0))
        self.came = came

    def next_step(self, after):
        step = 2 * self.step
        order = sorted(self.held)
        sums = call(
            functools.partial(add_kernel, len(order)),
            [shape(self.held[at].shape, bf16 if at & step else f32) for at in order],
            [self.held[at] for at in order] + [self.came[at] for at in order], "add", after,
        )
        self.held = dict(zip(order, sums))
        self.marker = sums[0]
        self.pass_on(step)


def opposite(one, two, after):
    rows, width = one.shape
    half = (rows // 2 + 15) // 16 * 16
    upper = call(functools.partial(relay_kernel, 0), shape((half, width), bf16), [two], "relay", after)
    lower = call(
        functools.partial(relay_kernel, half), shape((rows - half, width), bf16), [one], "relay", [upper]
    )
    lower = shifted(lower, "ctx", 2)
    return lower, shifted(upper, "ctx", 1)


def body(queries, keys, values, rates, w_gate, w_up, w_down, gains, out_proj):
    groups, rows, width = queries.shape
    hidden = w_gate.shape[2]
    chips = lax.axis_size("head") // 2
    acc_shape = shape((3, width, hidden), f32)
    weight_shapes = [shape((2 * width, 2 * hidden), bf16), shape((2 * width, hidden), bf16)]
    picked = shape((width, out_proj.shape[1] // 2), bf16)

    message = first_message(keys, values, rates)
    one, two = shifted(message, "ctx", 1), shifted(message, "ctx", 2)
    acc, *weights = call(
        first_grads_kernel, [acc_shape, *weight_shapes], [message, w_gate[0], w_up[0], w_down[0]], "grads"
    )
    own_proj, for_other = call(pick_kernel, [picked, picked], [out_proj], "pick", [acc])
    other_proj = shifted(for_other, "head", 1)
    local = call(
        local_band_kernel, shape((groups, rows - WINDOW, width), f32), [queries, keys, values],
        "local_band", [own_proj],
    )
    last = past = opposite(one, two, [local])

    totals = []
    combined = None
    for g in range(groups):
        if g > 0:
            acc = call(
                functools.partial(grads_kernel, 1, False), acc_shape, [message, *weights], "grads", [combined]
            )
            totals.append(HalvingSums(combined, own_proj, other_proj, [acc]))
            last = opposite(one, two, [totals[-1].marker])
        acc = call(
            functools.partial(grads_kernel, 2, True), acc_shape, [one, two, *weights, acc], "grads",
            [local] if g == 0 else [totals[-1].marker],
        )
        near, after = one, []
        if g < groups - 1:
            message = later_message(keys, values, rates, g + 1, [acc])
            one, two = shifted(message, "ctx", 1), shifted(message, "ctx", 2)
            after = [message]
        acc = call(
            functools.partial(last_grads_kernel, len(last)), acc_shape, [*last, *weights, acc], "grads", after,
            scratch=[pltpu.VMEM(message.shape, bf16)],
        )
        after = [acc]
        while g > 0 and totals[-1].held:
            totals[-1].next_step(after)
            after = [totals[-1].marker]
        outs, scratch = [shape((rows, width), bf16), *weight_shapes], []
        if g == groups - 1:
            outs, scratch = outs[:1], [pltpu.VMEM(kept.shape, kept.dtype) for kept in weight_shapes]
        combined, *weights = call(
            functools.partial(update_kernel, g, (1, len(last), len(past))), outs,
            [near, *last, *past, *weights, acc, queries, keys, values, local, gains],
            "update", after, flops=UPDATE_FLOPS if g < groups - 1 else 0, scratch=scratch,
        )
        past = last
    total = direct_sums(combined, own_proj, other_proj)
    finished = [
        call(finish_kernel, shape((rows, width), bf16), earlier.terms, "finish", total[:1]) for earlier in totals
    ]
    return call(
        functools.partial(finish_last_kernel, len(total)), shape((groups, rows, width), bf16),
        [*total, *finished], "finish_last", out=ANYWHERE,
        scratch=[pltpu.VMEM((rows, width), bf16), pltpu.SemaphoreType.DMA((groups - 1 + LAST_PIECES,))],
    )


def solution(mesh):
    return jax.shard_map(
        body,
        mesh=mesh,
        in_specs=(
            P(None, "ctx", "head"),
            P(None, "ctx", "head"),
            P(None, "ctx", "head"),
            P("head", None, "ctx"),
            P("head", None, None),
            P("head", None, None),
            P("head", None, None),
            P("head", None),
            P("head", None),
        ),
        out_specs=P(None, "ctx", "head"),
        check_vma=False,
    )
```

```python
import functools

import jax
import jax.numpy as jnp
from jax import lax
from jax.experimental import pallas as pl
from jax.experimental.pallas import tpu as pltpu
from jax.sharding import PartitionSpec as P

WINDOW = 256
NS_ITERS = 5
RATE_ROWS = 16
VMEM_LIMIT = 20 * 1024 * 1024
UPDATE_FLOPS = 30_000_000_000
LAST_PIECES = 4
MESSAGE_VMEM = 60 * 1024 * 1024

attn_temp = 5.0
step_size = 0.5
quintic_one = 3.4445
quintic_two = -4.775
quintic_three = 2.0315

f32 = jnp.float32
bf16 = jnp.bfloat16
NN = (((1,), (0,)), ((), ()))
NT = (((1,), (1,)), ((), ()))


def mm(left, right, dims=NN):
    return lax.dot_general(left, right, dims, preferred_element_type=f32)


def split(value):
    high = value.astype(bf16)
    return high, (value - high.astype(f32)).astype(bf16)


def cat(parts, axis):
    return jnp.concatenate(parts, axis=axis)


def mm_split(left, right):
    return mm(cat([left[0], left[0], left[1]], 1), cat([right[0], right[1], right[0]], 0))


def unit_scale(rows):
    wide = rows.astype(f32)
    return lax.rsqrt(jnp.sum(wide * wide, axis=-1, keepdims=True) + 1e-06)


def silu_parts(gate_pre):
    sigma = 0.5 * jnp.tanh(0.5 * gate_pre) + 0.5
    return sigma, gate_pre * sigma


def rate_column(packed, token_blocks):
    turned = packed.astype(f32).T
    columns = []
    for at in range(token_blocks):
        parts = [turned[:, at + token_blocks * piece : at + token_blocks * piece + 1] for piece in range(3)]
        columns.append(parts[0] + parts[1] + parts[2])
    return cat(columns, 0)


def stacked_split(value):
    return cat(split(value), 0)


def joined(stacked):
    rows = stacked.shape[0] // 2
    return stacked[:rows].astype(f32) + stacked[rows:].astype(f32)


TOKEN_TILE = 256


def add_messages(acc, messages, gate_up_ref, down_turned_ref):
    hidden_width = down_turned_ref.shape[1]
    block = min(256, hidden_width)
    blocks = [slice(at, at + block) for at in range(0, hidden_width, block)]
    sums = [[None if part is None else part[:, span] for span in blocks] for part in acc]
    tiles = []
    for message in messages:
        key_ref, value_ref, rate_ref = message_parts(message)
        count = value_ref.shape[0] // TOKEN_TILE
        rate = rate_column(rate_ref[...], count)
        for at in range(count):
            tiles.append((key_ref, value_ref, rate, slice(at * TOKEN_TILE, at * TOKEN_TILE + TOKEN_TILE)))
    state = [{} for _ in tiles]

    def forward(at):
        key_ref, value_ref, rate, rows = tiles[at]
        tile = state[at]
        keys, values = key_ref[rows], value_ref[rows]
        tile["rate"], tile["scale"] = rate[rows], unit_scale(keys)
        both_keys, both_values = cat([keys, keys], 1), cat([values, values], 1)
        tile["pre"] = []
        for span in blocks:
            gate_pre = mm(both_keys, gate_up_ref[:, span])
            yield
            up_pre = mm(both_keys, gate_up_ref[:, hidden_width + span.start : hidden_width + span.stop])
            yield
            tile["pre"].append((gate_pre, up_pre, mm(both_values, down_turned_ref[:, span])))
            yield
        tile["turned"] = [part.T for part in (keys, keys, values)]
        yield

    def middle(at):
        tile = state[at]
        tile["terms"] = []
        for gate_pre, up_pre, back in tile["pre"]:
            gate_pre, up_pre = gate_pre * tile["scale"], up_pre * tile["scale"]
            sigma, gate_act = silu_parts(gate_pre)
            back = back * (tile["rate"] * tile["scale"])
            slope = sigma + gate_act * (1.0 - sigma)
            terms = (back * up_pre * slope, back * gate_act, gate_act * up_pre * tile["rate"])
            tile["terms"].append([term.astype(bf16) for term in terms])
            yield

    def backward(at):
        tile = state[at]
        for column, terms in enumerate(tile["terms"]):
            for place, (left, right) in enumerate(zip(tile["turned"], terms)):
                part, before = mm(left, right), sums[place][column]
                sums[place][column] = part if before is None else before + part
                yield

    for step in range(len(tiles) + 2):
        stages = [
            stage(step - lag)
            for lag, stage in ((2, backward), (1, middle), (0, forward))
            if 0 <= step - lag < len(tiles)
        ]
        while stages:
            stages = [stage for stage in stages if next(stage, True) is None]
    for place in range(3):
        acc[place] = cat(sums[place], 1)


NS_PASSES = (1, 1, 3, 3, 3)


def parts_of(value, passes):
    return (value.astype(bf16),) if passes == 1 else split(value)


def plus_turned(matrix):
    return matrix + matrix.T


def gram_of(parts):
    whole = mm(parts[0], parts[0], NT)
    return whole if len(parts) == 1 else whole + plus_turned(mm(parts[0], parts[1], NT))


def square_of(parts):
    whole = mm(parts[0], parts[0])
    return whole if len(parts) == 1 else whole + plus_turned(mm(parts[0], parts[1]))


def product_of(left, right):
    return mm(left[0], right[0]) if len(left) == 1 else mm_split(left, right)


def orthogonal(grads, beside):
    iterates = [
        grad * (1.0 / (jnp.sqrt(jnp.sum(grad * grad, keepdims=True)) + 1e-06)) for grad in grads
    ]
    for passes in NS_PASSES:
        parts = [parts_of(iterate, passes) for iterate in iterates]
        grams = [gram_of(part) for part in parts]
        if passes > 1 and beside is not None:
            beside()
            beside = None
        squares = [square_of(parts_of(gram, passes)) for gram in grams]
        polys = [quintic_two * gram + quintic_three * square for gram, square in zip(grams, squares)]
        iterates = [
            quintic_one * iterate + product_of(parts_of(poly, passes), part)
            for iterate, poly, part in zip(iterates, polys, parts)
        ]
    return iterates


def band(query_rows, key_rows, value_rows, masked):
    query_half = (query_rows.astype(f32) * unit_scale(query_rows)).astype(bf16)
    key_half = (key_rows.astype(f32) * unit_scale(key_rows)).astype(bf16)
    scores = mm(query_half, key_half, NT)
    query_pos = lax.broadcasted_iota(jnp.int32, scores.shape, 0)
    key_pos = lax.broadcasted_iota(jnp.int32, scores.shape, 1)
    distance = query_pos + WINDOW - key_pos
    valid = (distance >= 0) & (distance < WINDOW)
    if masked is not None:
        valid = valid & ((key_pos >= WINDOW) | jnp.logical_not(masked))
    weights = jnp.where(valid, jnp.exp(attn_temp * (scores - 1.0)), 0.0)
    probs = (weights / jnp.sum(weights, axis=-1, keepdims=True)).astype(bf16)
    return mm(probs, value_rows)


def apply_fast(query_rows, gate_up, down_turned, gains):
    hidden_width = down_turned.shape[1]
    width = down_turned.shape[0] // 2
    pre = mm(cat([query_rows, query_rows], 1), gate_up) * unit_scale(query_rows)
    gate_pre, up_pre = pre[:, :hidden_width], pre[:, hidden_width:]
    high, low = split(silu_parts(gate_pre)[1] * up_pre)
    down_high, down_low = down_turned[:width], down_turned[width:]
    fast_out = mm(cat([high, high, low], 1), cat([down_high, down_low, down_high], 1), NT)
    mean_square = jnp.mean(fast_out * fast_out, axis=-1, keepdims=True)
    return fast_out * lax.rsqrt(mean_square + 1e-05) * gains


def rate_tile(rates_ref, group, blocks):
    left = [rates_ref[0, group : group + 1, at * 256 : at * 256 + 256] for at in range(blocks)]
    row_at = lax.broadcasted_iota(jnp.int32, (RATE_ROWS, 256), 0)
    tile = jnp.zeros((RATE_ROWS, 256), f32)
    for part in range(3):
        for at in range(blocks):
            rounded = left[at].astype(bf16).astype(f32)
            left[at] = left[at] - rounded
            tile = jnp.where(row_at == part * blocks + at, rounded, tile)
    return tile.astype(bf16)


def message_kernel(group, keys_ref, values_ref, rates_ref, out_ref):
    rows = keys_ref.shape[0]
    out_ref[:rows] = keys_ref[...]
    out_ref[rows : 2 * rows] = values_ref[...]
    out_ref[2 * rows :] = rate_tile(rates_ref, group, rows // 256)


def later_message_kernel(group, keys_ref, values_ref, rates_ref, out_ref):
    rows = keys_ref.shape[1]
    out_ref[:rows] = keys_ref[group]
    out_ref[rows : 2 * rows] = values_ref[group]
    out_ref[2 * rows :] = rate_tile(rates_ref, group, rows // 256)


def message_parts(message_ref):
    rows = (message_ref.shape[0] - RATE_ROWS) // 2
    return message_ref.at[:rows], message_ref.at[rows : 2 * rows], message_ref.at[2 * rows :]


def local_band_kernel(queries_ref, keys_ref, values_ref, out_ref):
    groups, rows, _ = queries_ref.shape
    for group in range(groups):
        for at in range(1, rows // WINDOW):
            upper = (at + 1) * WINDOW
            out_ref[group, at * WINDOW - WINDOW : at * WINDOW] = band(
                queries_ref[group, at * WINDOW : upper],
                keys_ref[group, upper - 2 * WINDOW : upper],
                values_ref[group, upper - 2 * WINDOW : upper],
                None,
            )


def first_grads_kernel(message, gate_ref, up_ref, down_ref, out_ref, gate_up_ref, down_turned_ref):
    gate_up_ref[...] = stacked_split(cat([gate_ref[...], up_ref[...]], 1))
    down_turned_ref[...] = stacked_split(down_ref[...].T)
    acc = [None] * 3
    add_messages(acc, [message], gate_up_ref, down_turned_ref)
    for at in range(3):
        out_ref[at] = acc[at]


def grads_kernel(chunks, carried, *refs):
    messages, refs = refs[:chunks], refs[chunks:]
    gate_up_ref, down_turned_ref = refs[:2]
    out_ref = refs[-1]
    acc = [refs[2][at] for at in range(3)] if carried else [None] * 3
    add_messages(acc, messages, gate_up_ref, down_turned_ref)
    for at in range(3):
        out_ref[at] = acc[at]


def last_grads_kernel(parts, *refs):
    gate_up_ref, down_turned_ref, acc_ref, out_ref, held = refs[parts:]
    start = 0
    for ref in reversed(refs[:parts]):
        held[start : start + ref.shape[0]] = ref[...]
        start += ref.shape[0]
    acc = [acc_ref[at] for at in range(3)]
    add_messages(acc, [held], gate_up_ref, down_turned_ref)
    for at in range(3):
        out_ref[at] = acc[at]


def tails(refs, rows):
    found = []
    for end in (rows, 2 * rows):
        for ref in reversed(refs):
            if end <= ref.shape[0]:
                found.append(ref[end - WINDOW : end])
                break
            end = end - ref.shape[0]
    return found


def update_kernel(group, counts, *refs):
    near, refs = refs[: counts[0]], refs[counts[0] :]
    last, refs = refs[: counts[1]], refs[counts[1] :]
    past, refs = refs[: counts[2]], refs[counts[2] :]
    gate_up_ref, down_turned_ref, acc_ref, queries_ref, keys_ref, values_ref, local_ref, gains_ref, *refs = refs
    out_ref, gate_up_out, down_turned_out = refs
    rows = queries_ref.shape[1]
    query_rows = queries_ref.at[group]
    place = lax.axis_index("ctx")
    is_first = place == 0
    is_near = lax.rem(place, 2) == 1
    halo = [jnp.where(is_near, *pair) for pair in zip(tails(near, rows), tails(last, rows))]
    if group > 0:
        halo = [jnp.where(is_first, *pair) for pair in zip(tails(past, rows), halo)]
    head_block = []

    def attend():
        head_block.append(band(
            query_rows[:WINDOW],
            cat([halo[0], keys_ref[group, :WINDOW]], 0),
            cat([halo[1], values_ref[group, :WINDOW]], 0),
            is_first if group == 0 else None,
        ))

    ortho = orthogonal([acc_ref[at] for at in range(3)], attend)
    gate_up_out[...] = stacked_split(joined(gate_up_ref) + step_size * cat(ortho[:2], 1))
    down_turned_out[...] = stacked_split(joined(down_turned_ref) + step_size * ortho[2])
    normed = apply_fast(query_rows[...], gate_up_out[...], down_turned_out[...], gains_ref[...])
    out_ref[:WINDOW] = (head_block[0] + normed[:WINDOW]).astype(bf16)
    if rows > WINDOW:
        out_ref[WINDOW:] = (local_ref[group] + normed[WINDOW:]).astype(bf16)


def pick_kernel(proj_ref, own_ref, other_ref):
    core = lax.rem(lax.axis_index("head"), 2)
    width = proj_ref.shape[0]
    for chip in range(own_ref.shape[1] // width):
        span = slice(chip * width, chip * width + width)
        for side, ref in ((core, own_ref), (1 - core, other_ref)):
            ref[:, span] = proj_ref[:, pl.ds(pl.multiple_of((2 * chip + side) * width, width), width)]


def relay_kernel(start, message_ref, part_ref):
    part_ref[...] = message_ref[start : start + part_ref.shape[0]]


def pair_kernel(own_ref, other_ref, own_proj, other_proj, kept_ref, *sent_refs):
    chip = lax.div(lax.axis_index("head"), 2)
    width = kept_ref.shape[1]
    both = cat([own_ref[...], other_ref[...]], 1)
    for step, ref in enumerate((kept_ref, *sent_refs)):
        span = pl.ds(pl.multiple_of((chip ^ step) * width, width), width)
        ref[...] = mm(both, cat([own_proj[:, span], other_proj[:, span]], 0)).astype(ref.dtype)


def own_part_kernel(own_ref, own_proj, *out_refs):
    chip = lax.div(lax.axis_index("head"), 2)
    width = own_ref.shape[1]
    for step, ref in enumerate(out_refs):
        span = pl.ds(pl.multiple_of((chip ^ step) * width, width), width)
        ref[...] = mm(own_ref[...], own_proj[:, span])


def other_part_kernel(chips, other_ref, other_proj, *refs):
    chip = lax.div(lax.axis_index("head"), 2)
    width = other_ref.shape[1]
    for step in range(chips):
        span = pl.ds(pl.multiple_of((chip ^ step) * width, width), width)
        ref = refs[chips + step]
        ref[...] = (refs[step][...] + mm(other_ref[...], other_proj[:, span])).astype(ref.dtype)


def total_of(refs):
    total = refs[0][...]
    for ref in refs[1:]:
        total = total + ref[...].astype(f32)
    return total.astype(bf16)


def add_kernel(count, *refs):
    for at in range(count):
        ref = refs[2 * count + at]
        ref[...] = (refs[at][...] + refs[count + at][...].astype(f32)).astype(ref.dtype)


def finish_kernel(*refs):
    refs[-1][...] = total_of(refs[:-1])


def finish_last_kernel(count, *refs):
    out_ref, held, sems = refs[-3:]
    terms, earlier = refs[:count], refs[count:-3]
    last = out_ref.shape[0] - 1
    copies = [
        pltpu.make_async_copy(ref, out_ref.at[at], sems.at[at]) for at, ref in enumerate(earlier)
    ]
    piece = held.shape[0] // LAST_PIECES
    for copy in copies:
        copy.start()
    for at in range(LAST_PIECES):
        rows = pl.ds(at * piece, piece)
        held[rows] = total_of([term.at[rows] for term in terms])
        copies.append(pltpu.make_async_copy(held.at[rows], out_ref.at[last, rows], sems.at[last + at]))
        copies[-1].start()
    for copy in copies:
        copy.wait()


VMEM = pl.BlockSpec(memory_space=pltpu.VMEM)
ANYWHERE = pl.BlockSpec(memory_space=pl.ANY)


def call(kernel, out_shape, operands, name, after=(), flops=0, scratch=(), out=VMEM):
    count = len(operands)

    def reading(*refs):
        kernel(*refs[:count], *refs[count + len(after) :])

    return pl.pallas_call(
        reading,
        out_shape=out_shape,
        in_specs=[VMEM] * count + [ANYWHERE] * len(after),
        out_specs=jax.tree.map(lambda _: out, out_shape),
        scratch_shapes=scratch,
        compiler_params=pltpu.CompilerParams(vmem_limit_bytes=VMEM_LIMIT),
        cost_estimate=pl.CostEstimate(flops=flops, bytes_accessed=0, transcendentals=0),
        name=name,
    )(*operands, *after)


def shape(dims, dtype):
    return jax.ShapeDtypeStruct(dims, dtype)


def first_message(keys, values, rates):
    _, rows, width = keys.shape
    dims = (2 * rows + RATE_ROWS, width)
    block = pl.BlockSpec((None, rows, width), lambda step: (0, 0, 0))
    return pl.pallas_call(
        functools.partial(message_kernel, 0),
        out_shape=shape(dims, bf16),
        grid=(1,),
        in_specs=[block, block, pl.BlockSpec(rates.shape, lambda step: (0, 0, 0))],
        out_specs=pl.BlockSpec(dims, lambda step: (0, 0)),
        compiler_params=pltpu.CompilerParams(vmem_limit_bytes=MESSAGE_VMEM),
        cost_estimate=pl.CostEstimate(flops=0, bytes_accessed=0, transcendentals=0),
        name="message",
    )(keys, values, rates)


def later_message(keys, values, rates, group, after):
    _, rows, width = keys.shape
    return call(
        functools.partial(later_message_kernel, group), shape((2 * rows + RATE_ROWS, width), bf16),
        [keys, values, rates], "message", after,
    )


def shifted(value, axis, step):
    count = lax.axis_size(axis)
    return lax.ppermute(value, axis, [(at, at ^ step) for at in range(count)])


def pair(combined, own_proj, other_proj, types, after=()):
    rows, width = combined.shape
    return call(
        pair_kernel, [shape((rows, width), kind) for kind in types],
        [combined, shifted(combined, "head", 1), own_proj, other_proj], "pair", after,
    )


def to_chip(block, step):
    return shifted(block, "head", 2 * step)


def direct_sums(combined, own_proj, other_proj):
    chips = lax.axis_size("head") // 2
    rows, width = combined.shape
    other = shifted(combined, "head", 1)
    parts = call(
        own_part_kernel, [shape((rows, width), f32)] * chips, [combined, own_proj], "own_part",
        flops=UPDATE_FLOPS,
    )
    kept, *sent = call(
        functools.partial(other_part_kernel, chips),
        [shape((rows, width), f32)] + [shape((rows, width), bf16)] * (chips - 1),
        [other, other_proj, *parts], "other_part",
    )
    order = [2, 1, *range(3, chips)]
    return [kept] + [to_chip(sent[step - 1], step) for step in order]


class HalvingSums:
    def __init__(self, combined, own_proj, other_proj, after):
        self.chips = lax.axis_size("head") // 2
        types = [bf16 if at % 2 else f32 for at in range(self.chips)]
        self.held = dict(enumerate(pair(combined, own_proj, other_proj, types, after)))
        self.terms = [self.held.pop(0)]
        self.marker = self.terms[0]
        self.pass_on(1)

    def pass_on(self, step):
        self.step = step
        sent = sorted((at for at in self.held if at & step), reverse=True)
        came = {at ^ step: to_chip(self.held.pop(at), step) for at in sent}
        self.terms.append(came.pop(0))
        self.came = came

    def next_step(self, after):
        step = 2 * self.step
        order = sorted(self.held)
        sums = call(
            functools.partial(add_kernel, len(order)),
            [shape(self.held[at].shape, bf16 if at & step else f32) for at in order],
            [self.held[at] for at in order] + [self.came[at] for at in order], "add", after,
        )
        self.held = dict(zip(order, sums))
        self.marker = sums[0]
        self.pass_on(step)


def opposite(one, two, after):
    rows, width = one.shape
    half = (rows // 2 + 15) // 16 * 16
    upper = call(functools.partial(relay_kernel, 0), shape((half, width), bf16), [two], "relay", after)
    lower = call(
        functools.partial(relay_kernel, half), shape((rows - half, width), bf16), [one], "relay", [upper]
    )
    lower = shifted(lower, "ctx", 2)
    return lower, shifted(upper, "ctx", 1)


def body(queries, keys, values, rates, w_gate, w_up, w_down, gains, out_proj):
    groups, rows, width = queries.shape
    hidden = w_gate.shape[2]
    chips = lax.axis_size("head") // 2
    acc_shape = shape((3, width, hidden), f32)
    weight_shapes = [shape((2 * width, 2 * hidden), bf16), shape((2 * width, hidden), bf16)]
    picked = shape((width, out_proj.shape[1] // 2), bf16)

    message = first_message(keys, values, rates)
    one, two = shifted(message, "ctx", 1), shifted(message, "ctx", 2)
    acc, *weights = call(
        first_grads_kernel, [acc_shape, *weight_shapes], [message, w_gate[0], w_up[0], w_down[0]], "grads"
    )
    own_proj, for_other = call(pick_kernel, [picked, picked], [out_proj], "pick", [acc])
    other_proj = shifted(for_other, "head", 1)
    local = call(
        local_band_kernel, shape((groups, rows - WINDOW, width), f32), [queries, keys, values],
        "local_band", [own_proj],
    )
    last = past = opposite(one, two, [local])

    totals = []
    combined = None
    for g in range(groups):
        if g > 0:
            acc = call(
                functools.partial(grads_kernel, 1, False), acc_shape, [message, *weights], "grads", [combined]
            )
            totals.append(HalvingSums(combined, own_proj, other_proj, [acc]))
            last = opposite(one, two, [totals[-1].marker])
        acc = call(
            functools.partial(grads_kernel, 2, True), acc_shape, [one, two, *weights, acc], "grads",
            [local] if g == 0 else [totals[-1].marker],
        )
        near, after = one, []
        if g < groups - 1:
            message = later_message(keys, values, rates, g + 1, [acc])
            one, two = shifted(message, "ctx", 1), shifted(message, "ctx", 2)
            after = [message]
        acc = call(
            functools.partial(last_grads_kernel, len(last)), acc_shape, [*last, *weights, acc], "grads", after,
            scratch=[pltpu.VMEM(message.shape, bf16)],
        )
        after = [acc]
        while g > 0 and totals[-1].held:
            totals[-1].next_step(after)
            after = [totals[-1].marker]
        outs, scratch = [shape((rows, width), bf16), *weight_shapes], []
        if g == groups - 1:
            outs, scratch = outs[:1], [pltpu.VMEM(kept.shape, kept.dtype) for kept in weight_shapes]
        combined, *weights = call(
            functools.partial(update_kernel, g, (1, len(last), len(past))), outs,
            [near, *last, *past, *weights, acc, queries, keys, values, local, gains],
            "update", after, flops=UPDATE_FLOPS if g < groups - 1 else 0, scratch=scratch,
        )
        past = last
    total = direct_sums(combined, own_proj, other_proj)
    finished = [
        call(finish_kernel, shape((rows, width), bf16), earlier.terms, "finish", total[:1]) for earlier in totals
    ]
    return call(
        functools.partial(finish_last_kernel, len(total)), shape((groups, rows, width), bf16),
        [*total, *finished], "finish_last", out=ANYWHERE,
        scratch=[pltpu.VMEM((rows, width), bf16), pltpu.SemaphoreType.DMA((groups - 1 + LAST_PIECES,))],
    )


def solution(mesh):
    return jax.shard_map(
        body,
        mesh=mesh,
        in_specs=(
            P(None, "ctx", "head"),
            P(None, "ctx", "head"),
            P(None, "ctx", "head"),
            P("head", None, "ctx"),
            P("head", None, None),
            P("head", None, None),
            P("head", None, None),
            P("head", None),
            P("head", None),
        ),
        out_specs=P(None, "ctx", "head"),
        check_vma=False,
    )
```

```python
import functools

import jax
import jax.numpy as jnp
from jax import lax
from jax.experimental import pallas as pl
from jax.experimental.pallas import tpu as pltpu
from jax.sharding import PartitionSpec as P

WINDOW = 256
NS_ITERS = 5
RATE_ROWS = 16
VMEM_LIMIT = 20 * 1024 * 1024
UPDATE_FLOPS = 30_000_000_000
LAST_PIECES = 4
MESSAGE_VMEM = 60 * 1024 * 1024

attn_temp = 5.0
step_size = 0.5
quintic_one = 3.4445
quintic_two = -4.775
quintic_three = 2.0315

f32 = jnp.float32
bf16 = jnp.bfloat16
NN = (((1,), (0,)), ((), ()))
NT = (((1,), (1,)), ((), ()))


def mm(left, right, dims=NN):
    return lax.dot_general(left, right, dims, preferred_element_type=f32)


def split(value):
    high = value.astype(bf16)
    return high, (value - high.astype(f32)).astype(bf16)


def cat(parts, axis):
    return jnp.concatenate(parts, axis=axis)


def mm_split(left, right):
    return mm(cat([left[0], left[0], left[1]], 1), cat([right[0], right[1], right[0]], 0))


def unit_scale(rows):
    wide = rows.astype(f32)
    return lax.rsqrt(jnp.sum(wide * wide, axis=-1, keepdims=True) + 1e-06)


def silu_parts(gate_pre):
    sigma = 0.5 * jnp.tanh(0.5 * gate_pre) + 0.5
    return sigma, gate_pre * sigma


def rate_column(packed, token_blocks):
    turned = packed.astype(f32).T
    columns = []
    for at in range(token_blocks):
        parts = [turned[:, at + token_blocks * piece : at + token_blocks * piece + 1] for piece in range(3)]
        columns.append(parts[0] + parts[1] + parts[2])
    return cat(columns, 0)


def stacked_split(value):
    return cat(split(value), 0)


def joined(stacked):
    rows = stacked.shape[0] // 2
    return stacked[:rows].astype(f32) + stacked[rows:].astype(f32)


TOKEN_TILE = 256


def add_messages(acc, messages, gate_up_ref, down_turned_ref):
    hidden_width = down_turned_ref.shape[1]
    block = min(256, hidden_width)
    blocks = [slice(at, at + block) for at in range(0, hidden_width, block)]
    sums = [[None if part is None else part[:, span] for span in blocks] for part in acc]
    tiles = []
    for message in messages:
        key_ref, value_ref, rate_ref = message_parts(message)
        count = value_ref.shape[0] // TOKEN_TILE
        rate = rate_column(rate_ref[...], count)
        for at in range(count):
            tiles.append((key_ref, value_ref, rate, slice(at * TOKEN_TILE, at * TOKEN_TILE + TOKEN_TILE)))
    state = [{} for _ in tiles]

    def forward(at):
        key_ref, value_ref, rate, rows = tiles[at]
        tile = state[at]
        keys, values = key_ref[rows], value_ref[rows]
        tile["rate"], tile["scale"] = rate[rows], unit_scale(keys)
        both_keys, both_values = cat([keys, keys], 1), cat([values, values], 1)
        tile["pre"] = []
        for span in blocks:
            gate_pre = mm(both_keys, gate_up_ref[:, span])
            yield
            up_pre = mm(both_keys, gate_up_ref[:, hidden_width + span.start : hidden_width + span.stop])
            yield
            tile["pre"].append((gate_pre, up_pre, mm(both_values, down_turned_ref[:, span])))
            yield
        tile["turned"] = [part.T for part in (keys, keys, values)]
        yield

    def middle(at):
        tile = state[at]
        tile["terms"] = []
        for gate_pre, up_pre, back in tile["pre"]:
            gate_pre, up_pre = gate_pre * tile["scale"], up_pre * tile["scale"]
            sigma, gate_act = silu_parts(gate_pre)
            back = back * (tile["rate"] * tile["scale"])
            slope = sigma + gate_act * (1.0 - sigma)
            terms = (back * up_pre * slope, back * gate_act, gate_act * up_pre * tile["rate"])
            tile["terms"].append([term.astype(bf16) for term in terms])
            yield

    def backward(at):
        tile = state[at]
        for column, terms in enumerate(tile["terms"]):
            for place, (left, right) in enumerate(zip(tile["turned"], terms)):
                part, before = mm(left, right), sums[place][column]
                sums[place][column] = part if before is None else before + part
                yield

    for step in range(len(tiles) + 2):
        stages = [
            stage(step - lag)
            for lag, stage in ((2, backward), (1, middle), (0, forward))
            if 0 <= step - lag < len(tiles)
        ]
        while stages:
            stages = [stage for stage in stages if next(stage, True) is None]
    for place in range(3):
        acc[place] = cat(sums[place], 1)


NS_PASSES = (1, 1, 3, 3, 3)


def parts_of(value, passes):
    return (value.astype(bf16),) if passes == 1 else split(value)


def plus_turned(matrix):
    return matrix + matrix.T


def gram_of(parts):
    if len(parts) == 1:
        return mm(parts[0], parts[0], NT)
    high, low = parts
    return plus_turned(mm(cat([high, high], 1), cat([high * 0.5, low], 1), NT))


def square_of(parts):
    if len(parts) == 1:
        return mm(parts[0], parts[0])
    high, low = parts
    return plus_turned(mm(cat([high, high], 1), cat([high * 0.5, low], 0)))


def product_of(left, right):
    return mm(left[0], right[0]) if len(left) == 1 else mm_split(left, right)


def orthogonal(grads, beside):
    iterates = [
        grad * (1.0 / (jnp.sqrt(jnp.sum(grad * grad, keepdims=True)) + 1e-06)) for grad in grads
    ]
    for passes in NS_PASSES:
        parts = [parts_of(iterate, passes) for iterate in iterates]
        grams = [gram_of(part) for part in parts]
        if passes > 1 and beside is not None:
            beside()
            beside = None
        squares = [square_of(parts_of(gram, passes)) for gram in grams]
        polys = [quintic_two * gram + quintic_three * square for gram, square in zip(grams, squares)]
        iterates = [
            quintic_one * iterate + product_of(parts_of(poly, passes), part)
            for iterate, poly, part in zip(iterates, polys, parts)
        ]
    return iterates


def band(query_rows, key_rows, value_rows, masked):
    query_half = (query_rows.astype(f32) * unit_scale(query_rows)).astype(bf16)
    key_half = (key_rows.astype(f32) * unit_scale(key_rows)).astype(bf16)
    scores = mm(query_half, key_half, NT)
    query_pos = lax.broadcasted_iota(jnp.int32, scores.shape, 0)
    key_pos = lax.broadcasted_iota(jnp.int32, scores.shape, 1)
    distance = query_pos + WINDOW - key_pos
    valid = (distance >= 0) & (distance < WINDOW)
    if masked is not None:
        valid = valid & ((key_pos >= WINDOW) | jnp.logical_not(masked))
    weights = jnp.where(valid, jnp.exp(attn_temp * (scores - 1.0)), 0.0)
    probs = (weights / jnp.sum(weights, axis=-1, keepdims=True)).astype(bf16)
    return mm(probs, value_rows)


def apply_fast(query_rows, gate_up, down_turned, gains):
    hidden_width = down_turned.shape[1]
    width = down_turned.shape[0] // 2
    pre = mm(cat([query_rows, query_rows], 1), gate_up) * unit_scale(query_rows)
    gate_pre, up_pre = pre[:, :hidden_width], pre[:, hidden_width:]
    high, low = split(silu_parts(gate_pre)[1] * up_pre)
    down_high, down_low = down_turned[:width], down_turned[width:]
    fast_out = mm(cat([high, high, low], 1), cat([down_high, down_low, down_high], 1), NT)
    mean_square = jnp.mean(fast_out * fast_out, axis=-1, keepdims=True)
    return fast_out * lax.rsqrt(mean_square + 1e-05) * gains


def rate_tile(rates_ref, group, blocks):
    left = [rates_ref[0, group : group + 1, at * 256 : at * 256 + 256] for at in range(blocks)]
    row_at = lax.broadcasted_iota(jnp.int32, (RATE_ROWS, 256), 0)
    tile = jnp.zeros((RATE_ROWS, 256), f32)
    for part in range(3):
        for at in range(blocks):
            rounded = left[at].astype(bf16).astype(f32)
            left[at] = left[at] - rounded
            tile = jnp.where(row_at == part * blocks + at, rounded, tile)
    return tile.astype(bf16)


def message_kernel(group, keys_ref, values_ref, rates_ref, out_ref):
    rows = keys_ref.shape[0]
    out_ref[:rows] = keys_ref[...]
    out_ref[rows : 2 * rows] = values_ref[...]
    out_ref[2 * rows :] = rate_tile(rates_ref, group, rows // 256)


def later_message_kernel(group, keys_ref, values_ref, rates_ref, out_ref):
    rows = keys_ref.shape[1]
    out_ref[:rows] = keys_ref[group]
    out_ref[rows : 2 * rows] = values_ref[group]
    out_ref[2 * rows :] = rate_tile(rates_ref, group, rows // 256)


def message_parts(message_ref):
    rows = (message_ref.shape[0] - RATE_ROWS) // 2
    return message_ref.at[:rows], message_ref.at[rows : 2 * rows], message_ref.at[2 * rows :]


def local_band_kernel(queries_ref, keys_ref, values_ref, out_ref):
    groups, rows, _ = queries_ref.shape
    for group in range(groups):
        for at in range(1, rows // WINDOW):
            upper = (at + 1) * WINDOW
            out_ref[group, at * WINDOW - WINDOW : at * WINDOW] = band(
                queries_ref[group, at * WINDOW : upper],
                keys_ref[group, upper - 2 * WINDOW : upper],
                values_ref[group, upper - 2 * WINDOW : upper],
                None,
            )


def first_grads_kernel(message, gate_ref, up_ref, down_ref, out_ref, gate_up_ref, down_turned_ref):
    gate_up_ref[...] = stacked_split(cat([gate_ref[...], up_ref[...]], 1))
    down_turned_ref[...] = stacked_split(down_ref[...].T)
    acc = [None] * 3
    add_messages(acc, [message], gate_up_ref, down_turned_ref)
    for at in range(3):
        out_ref[at] = acc[at]


def grads_kernel(chunks, carried, *refs):
    messages, refs = refs[:chunks], refs[chunks:]
    gate_up_ref, down_turned_ref = refs[:2]
    out_ref = refs[-1]
    acc = [refs[2][at] for at in range(3)] if carried else [None] * 3
    add_messages(acc, messages, gate_up_ref, down_turned_ref)
    for at in range(3):
        out_ref[at] = acc[at]


def last_grads_kernel(parts, *refs):
    gate_up_ref, down_turned_ref, acc_ref, out_ref, held = refs[parts:]
    start = 0
    for ref in reversed(refs[:parts]):
        held[start : start + ref.shape[0]] = ref[...]
        start += ref.shape[0]
    acc = [acc_ref[at] for at in range(3)]
    add_messages(acc, [held], gate_up_ref, down_turned_ref)
    for at in range(3):
        out_ref[at] = acc[at]


def tails(refs, rows):
    found = []
    for end in (rows, 2 * rows):
        for ref in reversed(refs):
            if end <= ref.shape[0]:
                found.append(ref[end - WINDOW : end])
                break
            end = end - ref.shape[0]
    return found


def update_kernel(group, counts, *refs):
    near, refs = refs[: counts[0]], refs[counts[0] :]
    last, refs = refs[: counts[1]], refs[counts[1] :]
    past, refs = refs[: counts[2]], refs[counts[2] :]
    gate_up_ref, down_turned_ref, acc_ref, queries_ref, keys_ref, values_ref, local_ref, gains_ref, *refs = refs
    out_ref, gate_up_out, down_turned_out = refs
    rows = queries_ref.shape[1]
    query_rows = queries_ref.at[group]
    place = lax.axis_index("ctx")
    is_first = place == 0
    is_near = lax.rem(place, 2) == 1
    halo = [jnp.where(is_near, *pair) for pair in zip(tails(near, rows), tails(last, rows))]
    if group > 0:
        halo = [jnp.where(is_first, *pair) for pair in zip(tails(past, rows), halo)]
    head_block = []

    def attend():
        head_block.append(band(
            query_rows[:WINDOW],
            cat([halo[0], keys_ref[group, :WINDOW]], 0),
            cat([halo[1], values_ref[group, :WINDOW]], 0),
            is_first if group == 0 else None,
        ))

    ortho = orthogonal([acc_ref[at] for at in range(3)], attend)
    gate_up_out[...] = stacked_split(joined(gate_up_ref) + step_size * cat(ortho[:2], 1))
    down_turned_out[...] = stacked_split(joined(down_turned_ref) + step_size * ortho[2])
    normed = apply_fast(query_rows[...], gate_up_out[...], down_turned_out[...], gains_ref[...])
    out_ref[:WINDOW] = (head_block[0] + normed[:WINDOW]).astype(bf16)
    if rows > WINDOW:
        out_ref[WINDOW:] = (local_ref[group] + normed[WINDOW:]).astype(bf16)


def pick_kernel(proj_ref, own_ref, other_ref):
    core = lax.rem(lax.axis_index("head"), 2)
    width = proj_ref.shape[0]
    for chip in range(own_ref.shape[1] // width):
        span = slice(chip * width, chip * width + width)
        for side, ref in ((core, own_ref), (1 - core, other_ref)):
            ref[:, span] = proj_ref[:, pl.ds(pl.multiple_of((2 * chip + side) * width, width), width)]


def relay_kernel(start, message_ref, part_ref):
    part_ref[...] = message_ref[start : start + part_ref.shape[0]]


def pair_kernel(own_ref, other_ref, own_proj, other_proj, kept_ref, *sent_refs):
    chip = lax.div(lax.axis_index("head"), 2)
    width = kept_ref.shape[1]
    both = cat([own_ref[...], other_ref[...]], 1)
    for step, ref in enumerate((kept_ref, *sent_refs)):
        span = pl.ds(pl.multiple_of((chip ^ step) * width, width), width)
        ref[...] = mm(both, cat([own_proj[:, span], other_proj[:, span]], 0)).astype(ref.dtype)


def own_part_kernel(own_ref, own_proj, *out_refs):
    chip = lax.div(lax.axis_index("head"), 2)
    width = own_ref.shape[1]
    for step, ref in enumerate(out_refs):
        span = pl.ds(pl.multiple_of((chip ^ step) * width, width), width)
        ref[...] = mm(own_ref[...], own_proj[:, span])


def other_part_kernel(chips, other_ref, other_proj, *refs):
    chip = lax.div(lax.axis_index("head"), 2)
    width = other_ref.shape[1]
    for step in range(chips):
        span = pl.ds(pl.multiple_of((chip ^ step) * width, width), width)
        ref = refs[chips + step]
        ref[...] = (refs[step][...] + mm(other_ref[...], other_proj[:, span])).astype(ref.dtype)


def total_of(refs):
    total = refs[0][...]
    for ref in refs[1:]:
        total = total + ref[...].astype(f32)
    return total.astype(bf16)


def add_kernel(count, *refs):
    for at in range(count):
        ref = refs[2 * count + at]
        ref[...] = (refs[at][...] + refs[count + at][...].astype(f32)).astype(ref.dtype)


def finish_kernel(*refs):
    refs[-1][...] = total_of(refs[:-1])


def finish_last_kernel(count, *refs):
    out_ref, held, sems = refs[-3:]
    terms, earlier = refs[:count], refs[count:-3]
    last = out_ref.shape[0] - 1
    copies = [
        pltpu.make_async_copy(ref, out_ref.at[at], sems.at[at]) for at, ref in enumerate(earlier)
    ]
    piece = held.shape[0] // LAST_PIECES
    for copy in copies:
        copy.start()
    for at in range(LAST_PIECES):
        rows = pl.ds(at * piece, piece)
        held[rows] = total_of([term.at[rows] for term in terms])
        copies.append(pltpu.make_async_copy(held.at[rows], out_ref.at[last, rows], sems.at[last + at]))
        copies[-1].start()
    for copy in copies:
        copy.wait()


VMEM = pl.BlockSpec(memory_space=pltpu.VMEM)
ANYWHERE = pl.BlockSpec(memory_space=pl.ANY)


def call(kernel, out_shape, operands, name, after=(), flops=0, scratch=(), out=VMEM):
    count = len(operands)

    def reading(*refs):
        kernel(*refs[:count], *refs[count + len(after) :])

    return pl.pallas_call(
        reading,
        out_shape=out_shape,
        in_specs=[VMEM] * count + [ANYWHERE] * len(after),
        out_specs=jax.tree.map(lambda _: out, out_shape),
        scratch_shapes=scratch,
        compiler_params=pltpu.CompilerParams(vmem_limit_bytes=VMEM_LIMIT),
        cost_estimate=pl.CostEstimate(flops=flops, bytes_accessed=0, transcendentals=0),
        name=name,
    )(*operands, *after)


def shape(dims, dtype):
    return jax.ShapeDtypeStruct(dims, dtype)


def first_message(keys, values, rates):
    _, rows, width = keys.shape
    dims = (2 * rows + RATE_ROWS, width)
    block = pl.BlockSpec((None, rows, width), lambda step: (0, 0, 0))
    return pl.pallas_call(
        functools.partial(message_kernel, 0),
        out_shape=shape(dims, bf16),
        grid=(1,),
        in_specs=[block, block, pl.BlockSpec(rates.shape, lambda step: (0, 0, 0))],
        out_specs=pl.BlockSpec(dims, lambda step: (0, 0)),
        compiler_params=pltpu.CompilerParams(vmem_limit_bytes=MESSAGE_VMEM),
        cost_estimate=pl.CostEstimate(flops=0, bytes_accessed=0, transcendentals=0),
        name="message",
    )(keys, values, rates)


def later_message(keys, values, rates, group, after):
    _, rows, width = keys.shape
    return call(
        functools.partial(later_message_kernel, group), shape((2 * rows + RATE_ROWS, width), bf16),
        [keys, values, rates], "message", after,
    )


def shifted(value, axis, step):
    count = lax.axis_size(axis)
    return lax.ppermute(value, axis, [(at, at ^ step) for at in range(count)])


def pair(combined, own_proj, other_proj, types, after=()):
    rows, width = combined.shape
    return call(
        pair_kernel, [shape((rows, width), kind) for kind in types],
        [combined, shifted(combined, "head", 1), own_proj, other_proj], "pair", after,
    )


def to_chip(block, step):
    return shifted(block, "head", 2 * step)


def direct_sums(combined, own_proj, other_proj):
    chips = lax.axis_size("head") // 2
    rows, width = combined.shape
    other = shifted(combined, "head", 1)
    parts = call(
        own_part_kernel, [shape((rows, width), f32)] * chips, [combined, own_proj], "own_part",
        flops=UPDATE_FLOPS,
    )
    kept, *sent = call(
        functools.partial(other_part_kernel, chips),
        [shape((rows, width), f32)] + [shape((rows, width), bf16)] * (chips - 1),
        [other, other_proj, *parts], "other_part",
    )
    order = [2, 1, *range(3, chips)]
    return [kept] + [to_chip(sent[step - 1], step) for step in order]


class HalvingSums:
    def __init__(self, combined, own_proj, other_proj, after):
        self.chips = lax.axis_size("head") // 2
        types = [bf16 if at % 2 else f32 for at in range(self.chips)]
        self.held = dict(enumerate(pair(combined, own_proj, other_proj, types, after)))
        self.terms = [self.held.pop(0)]
        self.marker = self.terms[0]
        self.pass_on(1)

    def pass_on(self, step):
        self.step = step
        sent = sorted((at for at in self.held if at & step), reverse=True)
        came = {at ^ step: to_chip(self.held.pop(at), step) for at in sent}
        self.terms.append(came.pop(0))
        self.came = came

    def next_step(self, after):
        step = 2 * self.step
        order = sorted(self.held)
        sums = call(
            functools.partial(add_kernel, len(order)),
            [shape(self.held[at].shape, bf16 if at & step else f32) for at in order],
            [self.held[at] for at in order] + [self.came[at] for at in order], "add", after,
        )
        self.held = dict(zip(order, sums))
        self.marker = sums[0]
        self.pass_on(step)


def opposite(one, two, after):
    rows, width = one.shape
    half = (rows // 2 + 15) // 16 * 16
    upper = call(functools.partial(relay_kernel, 0), shape((half, width), bf16), [two], "relay", after)
    lower = call(
        functools.partial(relay_kernel, half), shape((rows - half, width), bf16), [one], "relay", [upper]
    )
    lower = shifted(lower, "ctx", 2)
    return lower, shifted(upper, "ctx", 1)


def body(queries, keys, values, rates, w_gate, w_up, w_down, gains, out_proj):
    groups, rows, width = queries.shape
    hidden = w_gate.shape[2]
    chips = lax.axis_size("head") // 2
    acc_shape = shape((3, width, hidden), f32)
    weight_shapes = [shape((2 * width, 2 * hidden), bf16), shape((2 * width, hidden), bf16)]
    picked = shape((width, out_proj.shape[1] // 2), bf16)

    message = first_message(keys, values, rates)
    one, two = shifted(message, "ctx", 1), shifted(message, "ctx", 2)
    acc, *weights = call(
        first_grads_kernel, [acc_shape, *weight_shapes], [message, w_gate[0], w_up[0], w_down[0]], "grads"
    )
    own_proj, for_other = call(pick_kernel, [picked, picked], [out_proj], "pick", [acc])
    other_proj = shifted(for_other, "head", 1)
    local = call(
        local_band_kernel, shape((groups, rows - WINDOW, width), f32), [queries, keys, values],
        "local_band", [own_proj],
    )
    last = past = opposite(one, two, [local])

    totals = []
    combined = None
    for g in range(groups):
        if g > 0:
            acc = call(
                functools.partial(grads_kernel, 1, False), acc_shape, [message, *weights], "grads", [combined]
            )
            totals.append(HalvingSums(combined, own_proj, other_proj, [acc]))
            last = opposite(one, two, [totals[-1].marker])
        acc = call(
            functools.partial(grads_kernel, 2, True), acc_shape, [one, two, *weights, acc], "grads",
            [local] if g == 0 else [totals[-1].marker],
        )
        near, after = one, []
        if g < groups - 1:
            message = later_message(keys, values, rates, g + 1, [acc])
            one, two = shifted(message, "ctx", 1), shifted(message, "ctx", 2)
            after = [message]
        acc = call(
            functools.partial(last_grads_kernel, len(last)), acc_shape, [*last, *weights, acc], "grads", after,
            scratch=[pltpu.VMEM(message.shape, bf16)],
        )
        after = [acc]
        while g > 0 and totals[-1].held:
            totals[-1].next_step(after)
            after = [totals[-1].marker]
        outs, scratch = [shape((rows, width), bf16), *weight_shapes], []
        if g == groups - 1:
            outs, scratch = outs[:1], [pltpu.VMEM(kept.shape, kept.dtype) for kept in weight_shapes]
        combined, *weights = call(
            functools.partial(update_kernel, g, (1, len(last), len(past))), outs,
            [near, *last, *past, *weights, acc, queries, keys, values, local, gains],
            "update", after, flops=UPDATE_FLOPS if g < groups - 1 else 0, scratch=scratch,
        )
        past = last
    total = direct_sums(combined, own_proj, other_proj)
    finished = [
        call(finish_kernel, shape((rows, width), bf16), earlier.terms, "finish", total[:1]) for earlier in totals
    ]
    return call(
        functools.partial(finish_last_kernel, len(total)), shape((groups, rows, width), bf16),
        [*total, *finished], "finish_last", out=ANYWHERE,
        scratch=[pltpu.VMEM((rows, width), bf16), pltpu.SemaphoreType.DMA((groups - 1 + LAST_PIECES,))],
    )


def solution(mesh):
    return jax.shard_map(
        body,
        mesh=mesh,
        in_specs=(
            P(None, "ctx", "head"),
            P(None, "ctx", "head"),
            P(None, "ctx", "head"),
            P("head", None, "ctx"),
            P("head", None, None),
            P("head", None, None),
            P("head", None, None),
            P("head", None),
            P("head", None),
        ),
        out_specs=P(None, "ctx", "head"),
        check_vma=False,
    )
```
